1024 devices in a mesh: gz: 128 (over y_lo, z, core), gy: 8 (over x, y_hi).
Axes of the slice: x: 4, y: 4 (y_hi: 2, y_lo: 2; y = y_hi * 2 + y_lo), z: 32, core: 2. Of those that a mesh axis runs over, the one named last changes fastest.
Arguments:
- cell_type: int32 [2048, 3072], P('gz', 'gy'), may hold values from 0 to 3, as said below
- perturb: int32 [2048, 3072], P('gz', 'gy'), may hold values from -4 to 4
- velocity: float32 [3, 2048, 3072], P(None, 'gz', 'gy'), may hold values from -0.25 to 0.25
Outputs:
- temperature: float32 [2048, 3072], P('gz', 'gy')
- flow: float32 [3, 2048, 3072], P(None, 'gz', 'gy')
- nusselt: float32 [], replicated
The draws below stay inside these ranges and needn't reach their ends.
Inputs may be any that keep to these rules, and one draw needn't show every extreme that they name: `cell_type`: cells with x = 0, x = 23, z = 0 or z = 2047 are adiabatic walls unless y = 0 (hot) or y = 128 - 1 (cold); inside, a few scattered wall cells of all three kinds stand among fluid cells.
All inputs are finite; a program needn't handle non-finite values.
Results may differ from the reference program's by a relative error of at most 0.0003.
Values sent between devices are 32-bit elements; how exact they have to be, the bound alone decides.
No kernel may reach another device: no remote copies, remote signals or barrier semaphores. Data moves between devices by JAX's collectives and lax.ppermute only.
A program may use at most 32 MiB of HBM per device.

```python
import jax
import jax.numpy as jnp

NX = 24
STEPS = 8
NZ = 2048
NY = 128


def draw_cell_type(key, part):
    key = jax.random.fold_in(key, 7)
    rolls = jax.random.randint(key, (NZ, NY * NX), 0, 100)
    zpos = jnp.arange(NZ, dtype=jnp.int32)[:, None] + jnp.zeros((1, NY * NX), jnp.int32)
    flat = jnp.arange(NY * NX, dtype=jnp.int32)[None, :] + jnp.zeros((NZ, 1), jnp.int32)
    ypos = flat // NX
    xpos = flat % NX
    kinds = jnp.where(rolls < 3, rolls + 1, 0)
    edge = (xpos == 0) | (xpos == NX - 1) | (zpos == 0) | (zpos == NZ - 1)
    kinds = jnp.where(edge, 1, kinds)
    kinds = jnp.where(ypos == 0, 2, kinds)
    kinds = jnp.where(ypos == NY - 1, 3, kinds)
    return kinds.astype(jnp.int32)


def with_ends(array, key, smallest, top_value):
    place = [jax.random.randint(jax.random.fold_in(key, axis), (), 0, length) for axis, length in enumerate(array.shape)]
    longest = array.shape.index(max(array.shape))
    neighbour = place[:longest] + [(place[longest] + 1) % array.shape[longest]] + place[longest + 1:]
    return array.at[tuple(place)].set(smallest).at[tuple(neighbour)].set(top_value)


def block_levels(rng, shape, cuts, least, largest):
    def one(position, parts):
        steps = jax.random.uniform(jax.random.fold_in(jax.random.fold_in(rng, 6), position), (parts,), jnp.float32, least / len(cuts), largest / len(cuts))
        return jnp.repeat(jnp.exp(steps), shape[position] // parts).reshape((-1,) + (1,) * (len(shape) - position - 1))

    gain = one(*cuts[0])
    for cut in cuts[1:]:
        gain = gain * one(*cut)
    return gain


def normal_values(rng, dims, width, reach, shards=(), kind=jnp.bfloat16):
    values = width * jax.random.normal(rng, dims, jnp.float32)
    if shards:
        values = values * block_levels(rng, dims, shards, -0.22, 0.18)
    return jnp.clip(values, -reach, reach).astype(kind)


def setup_inputs(seed: int = 0) -> dict:
    keys = jax.random.split(jax.random.key(seed), 4)
    return {
        "cell_type": draw_cell_type(jax.random.fold_in(keys[3], 71), 0),
        "perturb": with_ends(jax.random.randint(keys[1], (NZ, NY * NX), -4, 5), jax.random.fold_in(keys[1], 1), -4, 4).astype(jnp.int32),
        "velocity": normal_values(keys[2], (3, NZ, NY * NX), 0.1, 0.25, ((1, 128), (2, 8)), jnp.float32),
    }


TAU_F = 0.52
TAU_G = 0.5376

LAT19 = [(0, 0, 0), (1, 0, 0), (-1, 0, 0), (0, 1, 0), (0, -1, 0), (0, 0, 1), (0, 0, -1),
         (1, 1, 0), (-1, -1, 0), (1, -1, 0), (-1, 1, 0), (1, 0, 1), (-1, 0, -1), (1, 0, -1),
         (-1, 0, 1), (0, 1, 1), (0, -1, -1), (0, 1, -1), (0, -1, 1)]
WGT19 = [1.0 / 3.0] + [1.0 / 18.0] * 6 + [1.0 / 36.0] * 12
LAT7 = LAT19[:7]
WGT7 = [0.25] + [0.125] * 6


def opposite(table, index):
    back = tuple(-v for v in table[index])
    return table.index(back)


def build_state(cell_type, perturb, velocity, zpos, height):
    fluid = cell_type == 0
    speeds = [jnp.where(fluid, velocity[a], 0.0) for a in range(3)]
    base = 0.5 - 0.75 * (zpos + 0.5) / height + 0.05 * perturb.astype(jnp.float32)
    walls = jnp.where(cell_type == 2, 0.5, jnp.where(cell_type == 3, -0.5, 0.0))
    temp = jnp.where(fluid, base, walls).astype(jnp.float32)
    usq = speeds[0] ** 2 + speeds[1] ** 2 + speeds[2] ** 2
    chans = []
    for i in range(19):
        cvec = LAT19[i]
        proj = cvec[0] * speeds[0] + cvec[1] * speeds[1] + cvec[2] * speeds[2]
        chans.append(WGT19[i] * (1.0 + 3.0 * proj + 4.5 * proj * proj - 1.5 * usq))
    for j in range(7):
        cvec = LAT7[j]
        proj = cvec[0] * speeds[0] + cvec[1] * speeds[1] + cvec[2] * speeds[2]
        chans.append(WGT7[j] * temp * (1.0 + 4.0 * proj))
    chans.append((cell_type + 1).astype(jnp.float32))
    return jnp.stack(chans).astype(jnp.float32)


def moments(state):
    kind = state[26]
    fluid = kind == 1.0
    rho = sum(state[i] for i in range(19))
    safe = jnp.where(fluid, rho, 1.0)
    speeds = [sum(LAT19[i][a] * state[i] for i in range(19) if LAT19[i][a] != 0) / safe for a in range(3)]
    speeds = [jnp.where(fluid, s, 0.0) for s in speeds]
    temp = sum(state[19 + j] for j in range(7))
    return rho, speeds, temp, fluid


def collide_stream(state, depth_cells):
    rho, speeds, temp, fluid = moments(state)
    usq = speeds[0] ** 2 + speeds[1] ** 2 + speeds[2] ** 2
    post = []
    for i in range(19):
        cvec = LAT19[i]
        proj = cvec[0] * speeds[0] + cvec[1] * speeds[1] + cvec[2] * speeds[2]
        equil = WGT19[i] * rho * (1.0 + 3.0 * proj + 4.5 * proj * proj - 1.5 * usq)
        post.append(state[i] + (equil - state[i]) / TAU_F)
    for j in range(7):
        cvec = LAT7[j]
        proj = cvec[0] * speeds[0] + cvec[1] * speeds[1] + cvec[2] * speeds[2]
        equil = WGT7[j] * temp * (1.0 + 4.0 * proj)
        post.append(state[19 + j] + (equil - state[19 + j]) / TAU_G)
    post.append(state[26])
    post = jnp.stack(post)
    padded = jnp.pad(post, ((0, 0), (0, 0), (1, 1)))
    zcount = state.shape[1] - 2
    lcount = state.shape[2] - 2 * depth_cells

    def source(chan, cvec):
        offset = cvec[1] * depth_cells + cvec[0]
        zlow = 1 - cvec[2]
        llow = depth_cells + 1 - offset
        return padded[chan, zlow:zlow + zcount, llow:llow + lcount]

    center = post[:, 1:1 + zcount, depth_cells:depth_cells + lcount]
    before = state[:, 1:1 + zcount, depth_cells:depth_cells + lcount]
    cfluid = center[26] == 1.0
    result = []
    for i in range(19):
        skind = source(26, LAT19[i])
        moved = jnp.where(skind == 1.0, source(i, LAT19[i]), center[opposite(LAT19, i)])
        result.append(jnp.where(cfluid, moved, before[i]))
    for j in range(7):
        skind = source(26, LAT7[j])
        bounce = center[19 + opposite(LAT7, j)]
        hotside = skind == 3.0
        coldside = skind == 4.0
        wall_temp = jnp.where(hotside, 0.5, -0.5)
        anti = -bounce + 2.0 * WGT7[j] * wall_temp
        moved = jnp.where(skind == 1.0, source(19 + j, LAT7[j]),
                          jnp.where(hotside | coldside, anti, bounce))
        result.append(jnp.where(cfluid, moved, before[19 + j]))
    result.append(center[26])
    return jnp.stack(result)


def hot_terms(previous, final_state, depth_cells):
    zcount = final_state.shape[1]
    lcount = final_state.shape[2]
    below_hot = previous[26, 1:1 + zcount, 0:lcount] == 3.0
    rho, speeds, temp, fluid = moments(final_state)
    return jnp.sum(jnp.where(fluid & below_hot, 0.5 - temp, 0.0)), temp, speeds


def reference(cell_type, perturb, velocity):
    zpos = jnp.arange(NZ, dtype=jnp.float32)[:, None]
    state = build_state(cell_type, perturb, velocity, zpos, NZ)
    previous = state
    for step in range(STEPS):
        previous = jnp.pad(state, ((0, 0), (1, 1), (NX, NX)))
        state = collide_stream(previous, NX)
    total, temp, speeds = hot_terms(previous, state, NX)
    nusselt = total * (2.0 / (NX * NZ))
    return temp, jnp.stack(speeds), nusselt.astype(jnp.float32)
```

```python
import numpy as np

import jax
import jax.numpy as jnp
from jax import lax
from jax.experimental import pallas as pl
from jax.experimental.pallas import tpu as pltpu
from jax.sharding import Mesh, PartitionSpec as P

NX = 24
STEPS = 8
HALO = STEPS
TAU_F = 0.52
TAU_G = 0.5376
LAT19 = [
    (0, 0, 0),
    (1, 0, 0),
    (-1, 0, 0),
    (0, 1, 0),
    (0, -1, 0),
    (0, 0, 1),
    (0, 0, -1),
    (1, 1, 0),
    (-1, -1, 0),
    (1, -1, 0),
    (-1, 1, 0),
    (1, 0, 1),
    (-1, 0, -1),
    (1, 0, -1),
    (-1, 0, 1),
    (0, 1, 1),
    (0, -1, -1),
    (0, 1, -1),
    (0, -1, 1),
]
WGT19 = [1.0 / 3.0] + [1.0 / 18.0] * 6 + [1.0 / 36.0] * 12
LAT7 = LAT19[:7]
WGT7 = [0.25] + [0.125] * 6
OPP = [LAT19.index(tuple(-v for v in c)) for c in LAT19]

KAPPA = -1.0 / (1.0 - TAU_F)
W2 = KAPPA / 36.0
OMG = 1.0 / TAU_G
LAMG = 1.0 - OMG
BIG = 1e30

NS = 8
XT = NX // 8
ROWS = 40


def shift_lanes(v, by):
    return pltpu.roll(v, by % 128, axis=1)


def tile(ref, chan, s, xt, cvec=(0, 0, 0)):
    v = ref[chan, s + 1 - cvec[1], pl.ds(8 + 8 * xt - cvec[0], 8), :]
    return shift_lanes(v, cvec[2]) if cvec[2] else v


def put(ref, chan, s, xt, v):
    ref[chan, s + 1, pl.ds(8 + 8 * xt, 8), :] = v


def wrap(ref, chan, low, high):
    for xt in range(XT):
        rows = pl.ds(8 + 8 * xt, 8)
        if low:
            ref[chan, 0, rows, :] = shift_lanes(ref[chan, NS, rows, :], 32)
        if high:
            ref[chan, NS + 1, rows, :] = shift_lanes(ref[chan, 1, rows, :], -32)


def moments(f):
    quad = []
    for k in (7, 11, 15):
        p, m = f[k] + f[k + 2], f[k + 1] + f[k + 3]
        quad.append((p + m, p - m, (f[k] - f[k + 2]) - (f[k + 1] - f[k + 3])))
    rho = f[0] + (f[1] + f[2]) + (f[3] + f[4]) + (f[5] + f[6])
    rho = rho + quad[0][0] + quad[1][0] + quad[2][0]
    mx = (f[1] - f[2]) + quad[0][1] + quad[1][1]
    my = (f[3] - f[4]) + quad[0][2] + quad[2][1]
    mz = (f[5] - f[6]) + quad[1][2] + quad[2][2]
    return rho, mx, my, mz


def inverse(v):
    r = pl.reciprocal(v, approx=True)
    return r * (2.0 - v * r)


def collide(f, g):
    rho, mx, my, mz = moments(f)
    inv = inverse(rho)
    mom = (mx, my, mz)
    u = [m * inv for m in mom]
    y = [(4.5 * W2) * m for m in mom]
    diag = [y[a] * u[a] for a in range(3)]
    o = [(3.0 * W2) * m for m in mom]
    base = W2 * rho - (diag[0] + diag[1] + diag[2]) * (1.0 / 3.0)
    t = [base + d for d in diag]
    post = [None] * 19
    post[0] = f[0] + 12.0 * base
    for a in range(3):
        e, od = t[a] + t[a], o[a] + o[a]
        post[1 + 2 * a] = f[1 + 2 * a] + (e + od)
        post[2 + 2 * a] = f[2 + 2 * a] + (e - od)
    for k, a, b in ((7, 0, 1), (11, 0, 2), (15, 1, 2)):
        e = t[a] + diag[b]
        cross = (y[a] + y[a]) * u[b]
        ep, em = e + cross, e - cross
        op, om = o[a] + o[b], o[a] - o[b]
        post[k] = f[k] + (ep + op)
        post[k + 1] = f[k + 1] + (ep - op)
        post[k + 2] = f[k + 2] + (em + om)
        post[k + 3] = f[k + 3] + (em - om)
    temp = g[0] + (g[1] + g[2]) + (g[3] + g[4]) + (g[5] + g[6])
    eq = (0.125 * OMG) * temp
    eq4 = (0.5 * OMG) * temp
    post.append(LAMG * g[0] + (eq + eq))
    for a in range(3):
        ua = eq4 * u[a]
        post.append(LAMG * g[1 + 2 * a] + (eq + ua))
        post.append(LAMG * g[2 + 2 * a] + (eq - ua))
    return post


def stream(src, wa, wb, s, xt):
    f = [tile(src, 0, s, xt)]
    g = [tile(src, 19, s, xt)]
    for i in range(1, 19):
        moved = tile(src, i, s, xt, LAT19[i])
        open_ = moved < BIG
        f.append(jnp.where(open_, moved, tile(src, OPP[i], s, xt)))
        if i < 7:
            back = tile(src, 19 + OPP[i], s, xt)
            coeff = pl.ds(8 * xt, 8)
            back = wa[i - 1, s, coeff, :] * back + wb[i - 1, s, coeff, :]
            g.append(jnp.where(open_, tile(src, 19 + i, s, xt, LAT19[i]), back))
    return f, g


def window(zbase, left, own, right, top, bot, temp_out, flow_out, part_out,
           stage, inp, kinds, pops, wa, wb, res):
    height = zbase[1]
    for a in range(5):
        blocks = (left[a], own[a, :, 0:192], own[a, :, 192:384], right[a])
        for q in range(4):
            r0 = 32 * q
            stage[a, r0 : r0 + 8, 0:192] = top[a, :, 192 * q : 192 * q + 192]
            stage[a, r0 + 8 : r0 + 24, 0:192] = blocks[q]
            stage[a, r0 + 24 : r0 + 32, 0:192] = bot[a, :, 192 * q : 192 * q + 192]
        inp[a, 0:16] = stage[a, :, 0:128].T.reshape(16, 8, 128)
        inp[a, 16:24] = stage[a, :, 128:256].T[0:64].reshape(8, 8, 128)

    lane = lax.broadcasted_iota(jnp.int32, (8, 128), 1)
    zin = lane % 32
    mine = (zin >= HALO) & (zin < 32 - HALO) & (lane >= 32) & (lane < 96)
    zpos = zbase[0] + zin.astype(jnp.float32)
    ramp = 0.5 - 0.75 * (zpos + 0.5) / height

    def first(s, carry):
        for xt in range(XT):
            kind = inp[0, s * XT + xt]
            put(kinds, 0, s, xt, kind)
            fluid = kind == 0.0
            u = [jnp.where(fluid, inp[2 + a, s * XT + xt], 0.0) for a in range(3)]
            walls = jnp.where(kind == 2.0, 0.5, jnp.where(kind == 3.0, -0.5, 0.0))
            temp = jnp.where(fluid, ramp + 0.05 * inp[1, s * XT + xt], walls)
            usq = u[0] * u[0] + u[1] * u[1] + u[2] * u[2]
            f, g = [], []
            for i in range(19):
                c = LAT19[i]
                if i == 0:
                    f.append(jnp.where(fluid, WGT19[0] * (1.0 - 1.5 * usq), jnp.nan))
                    g.append(WGT7[0] * temp)
                    continue
                proj = sum(u[a] if c[a] > 0 else -u[a] for a in range(3) if c[a])
                f.append(WGT19[i] * (1.0 + 3.0 * proj + 4.5 * proj * proj - 1.5 * usq))
                if i < 7:
                    g.append(WGT7[i] * temp * (1.0 + 4.0 * proj))
            for chan, v in enumerate(collide(f, g)):
                put(pops.at[0], chan, s, xt, v)
        return carry

    lax.fori_loop(0, NS, first, 0)
    wrap(kinds, 0, True, True)

    def edges(dst):
        for i in range(1, 19):
            if LAT19[i][1]:
                wrap(dst, i, LAT19[i][1] > 0, LAT19[i][1] < 0)
                if i < 7:
                    wrap(dst, 19 + i, LAT19[i][1] > 0, LAT19[i][1] < 0)

    edges(pops.at[0])

    def walls_of(s, carry):
        for xt in range(XT):
            rows = pl.ds(8 * xt, 8)
            for i in range(1, 7):
                near = tile(kinds, 0, s, xt, LAT19[i])
                hot, cold = near == 2.0, near == 3.0
                wa[i - 1, s, rows, :] = jnp.where(hot | cold, -1.0, 1.0)
                wb[i - 1, s, rows, :] = jnp.where(hot, 0.125, jnp.where(cold, -0.125, 0.0))
        return carry

    lax.fori_loop(0, NS, walls_of, 0)

    def step(k, carry):
        src, dst = pops.at[lax.rem(k + 1, 2)], pops.at[lax.rem(k, 2)]

        def line(s, c):
            for xt in range(XT):
                f, g = stream(src, wa, wb, s, xt)
                for chan, v in enumerate(collide(f, g)):
                    put(dst, chan, s, xt, v)
            return c

        lax.fori_loop(0, NS, line, 0)
        edges(dst)
        return carry

    lax.fori_loop(1, STEPS, step, 0)
    src = pops.at[(STEPS - 1) % 2]

    def last(s, total):
        for xt in range(XT):
            f, g = stream(src, wa, wb, s, xt)
            rho, mx, my, mz = moments(f)
            fluid = f[0] < BIG
            inv = inverse(rho)
            kind = tile(kinds, 0, s, xt)
            walls = jnp.where(kind == 2.0, 0.5, jnp.where(kind == 3.0, -0.5, 0.0))
            temp = g[0] + (g[1] + g[2]) + (g[3] + g[4]) + (g[5] + g[6])
            temp = jnp.where(fluid, temp, walls)
            res[0, s * XT + xt] = temp
            for a, m in enumerate((mx, my, mz)):
                res[1 + a, s * XT + xt] = jnp.where(fluid, m * inv, 0.0)
            heated = fluid & mine & (tile(kinds, 0, s, xt, (0, 1, 0)) == 2.0)
            total = total + jnp.where(heated, 0.5 - temp, 0.0)
        return total

    total = lax.fori_loop(0, NS, last, jnp.zeros((8, 128), jnp.float32))
    part_out[...] = jnp.full(part_out.shape, jnp.sum(total), jnp.float32)
    for o in range(4):
        one = res[o, 0:16].reshape(128, 128).T
        two = res[o, 16:32].reshape(128, 128).T
        for q in (1, 2):
            rows = slice(32 * q + 8, 32 * q + 24)
            at = 192 * (q - 1)
            val = jnp.concatenate([one[rows], two[rows, 0:64]], axis=1)
            if o == 0:
                temp_out[:, at : at + 192] = val
            else:
                flow_out[o - 1, :, at : at + 192] = val


def all_sum(part, axes, count):
    return jnp.sum(lax.all_to_all(part, axes, 0, 0, tiled=True), axis=0)


def make_body(gz, gy, near, far, n_near, n_far, n_gz, n_gy):
    def body(cell_type, perturb, velocity):
        slab, cells = cell_type.shape
        height = slab * n_gz
        own = jnp.concatenate(
            [
                cell_type.astype(jnp.float32)[None],
                perturb.astype(jnp.float32)[None],
                velocity,
            ]
        )
        rim = HALO * NX
        up = [(i, (i + 1) % n_gy) for i in range(n_gy)]
        down = [((i + 1) % n_gy, i) for i in range(n_gy)]
        left = lax.ppermute(own[:, :, cells - rim :], gy, up)
        right = lax.ppermute(own[:, :, :rim], gy, down)
        wide = jnp.concatenate([left, own, right], axis=2)
        up = [(i, (i + 1) % n_gz) for i in range(n_gz)]
        down = [((i + 1) % n_gz, i) for i in range(n_gz)]
        top = lax.ppermute(wide[:, slab - HALO :], gz, up)
        bot = lax.ppermute(wide[:, :HALO], gz, down)
        zbase = jnp.stack(
            [
                (lax.axis_index(gz) * slab - HALO).astype(jnp.float32),
                jnp.float32(height),
            ]
        )
        vmem = pl.BlockSpec(memory_space=pltpu.VMEM)
        f32 = jnp.float32
        temp, flow, part = pl.pallas_call(
            window,
            in_specs=[pl.BlockSpec(memory_space=pltpu.SMEM)] + [vmem] * 5,
            out_specs=[vmem] * 3,
            out_shape=[
                jax.ShapeDtypeStruct((slab, cells), f32),
                jax.ShapeDtypeStruct((3, slab, cells), f32),
                jax.ShapeDtypeStruct((n_near, 128), f32),
            ],
            scratch_shapes=[
                pltpu.VMEM((5, 128, 256), f32),
                pltpu.VMEM((5, NS * XT, 8, 128), f32),
                pltpu.VMEM((1, NS + 2, ROWS, 128), f32),
                pltpu.VMEM((2, 26, NS + 2, ROWS, 128), f32),
                pltpu.VMEM((6, NS, NX, 128), f32),
                pltpu.VMEM((6, NS, NX, 128), f32),
                pltpu.VMEM((4, 32, 8, 128), f32),
            ],
            compiler_params=pltpu.CompilerParams(vmem_limit_bytes=40 * 1024 * 1024),
            name="lattice_window",
        )(zbase, left, own, right, top, bot)
        line = all_sum(part, near, n_near)
        line = all_sum(jnp.broadcast_to(line, (n_far, 128)), far, n_far)
        return temp, flow, line[0] * (2.0 / (NX * height))

    return body


def solution(mesh):
    n_gz, n_gy = mesh.shape["gz"], mesh.shape["gy"]
    z = n_gz // 4
    fine = Mesh(
        np.asarray(mesh.devices).reshape(2, z, 2, n_gy),
        ("yl", "z", "core", "gy"),
    )
    gz = ("yl", "z", "core")
    near = ("yl", "core", "gy")
    body = make_body(gz, "gy", near, "z", 4 * n_gy, z, n_gz, n_gy)
    return jax.shard_map(
        body,
        mesh=fine,
        in_specs=(P(gz, "gy"), P(gz, "gy"), P(None, gz, "gy")),
        out_specs=(P(gz, "gy"), P(None, gz, "gy"), P()),
        check_vma=False,
    )
```

```python
import numpy as np

import jax
import jax.numpy as jnp
from jax import lax
from jax.experimental import pallas as pl
from jax.experimental.pallas import tpu as pltpu
from jax.sharding import Mesh, PartitionSpec as P

NX = 24
STEPS = 8
HALO = STEPS
TAU_F = 0.52
TAU_G = 0.5376
LAT19 = [
    (0, 0, 0),
    (1, 0, 0),
    (-1, 0, 0),
    (0, 1, 0),
    (0, -1, 0),
    (0, 0, 1),
    (0, 0, -1),
    (1, 1, 0),
    (-1, -1, 0),
    (1, -1, 0),
    (-1, 1, 0),
    (1, 0, 1),
    (-1, 0, -1),
    (1, 0, -1),
    (-1, 0, 1),
    (0, 1, 1),
    (0, -1, -1),
    (0, 1, -1),
    (0, -1, 1),
]
WGT19 = [1.0 / 3.0] + [1.0 / 18.0] * 6 + [1.0 / 36.0] * 12
LAT7 = LAT19[:7]
WGT7 = [0.25] + [0.125] * 6
OPP = [LAT19.index(tuple(-v for v in c)) for c in LAT19]

KAPPA = -1.0 / (1.0 - TAU_F)
W2 = KAPPA / 36.0
KAPPA_0 = 1.0 / 36.0 / (1.0 - 1.0 / TAU_F)
OMG = 1.0 / TAU_G
LAMG = 1.0 - OMG
BIG = 1e30

NS = 8
XT = NX // 8
ROWS = 40


COPY = list(range(26))
for _i in range(1, 19):
    if LAT19[_i][2]:
        COPY[_i] = 26 + sum(1 for c in COPY if c >= 26)
for _i in range(1, 7):
    if LAT19[_i][2]:
        COPY[19 + _i] = 26 + sum(1 for c in COPY if c >= 26)
NCHAN = 26 + sum(1 for c in COPY if c >= 26)


def shift_lanes(v, by):
    return pltpu.roll(v, by % 128, axis=1)


def velocity_of(chan):
    return LAT19[chan] if chan < 19 else LAT19[chan - 19]


def put(ref, chan, slot, xt, v):
    ref[chan, slot, pl.ds(8 + 8 * xt, 8), :] = v


def tile(ref, chan, s, xt):
    return ref[chan, s + 1, pl.ds(8 + 8 * xt, 8), :]


def moved_tile(ref, chan, s, xt):
    c = velocity_of(chan)
    return ref[COPY[chan], s + 1 - c[1], pl.ds(8 + 8 * xt - c[0], 8), :]


def put_all(ref, s, xt, post):
    for chan, v in enumerate(post):
        put(ref, chan, s + 1, xt, v)


def copies(ref):
    def roll_line(s, carry):
        for xt in range(XT):
            for chan in range(26):
                c = velocity_of(chan)
                if c[2]:
                    put(ref, COPY[chan], s + 1, xt, shift_lanes(tile(ref, chan, s, xt), c[2]))
        return carry

    for xt in range(XT):
        for chan in range(26):
            c = velocity_of(chan)
            if c[1] > 0:
                put(ref, COPY[chan], 0, xt, shift_lanes(tile(ref, chan, NS - 1, xt), c[2] + 32))
            if c[1] < 0:
                put(ref, COPY[chan], NS + 1, xt, shift_lanes(tile(ref, chan, 0, xt), c[2] - 32))
    lax.fori_loop(0, NS, roll_line, 0, unroll=True)


def moments(f):
    quad = []
    for k in (7, 11, 15):
        p, m = f[k] + f[k + 2], f[k + 1] + f[k + 3]
        quad.append((p + m, p - m, (f[k] - f[k + 2]) - (f[k + 1] - f[k + 3])))
    rho = f[0] + (f[1] + f[2]) + (f[3] + f[4]) + (f[5] + f[6])
    rho = rho + quad[0][0] + quad[1][0] + quad[2][0]
    mx = (f[1] - f[2]) + quad[0][1] + quad[1][1]
    my = (f[3] - f[4]) + quad[0][2] + quad[2][1]
    mz = (f[5] - f[6]) + quad[1][2] + quad[2][2]
    return rho, mx, my, mz


def inverse(v):
    r = pl.reciprocal(v, approx=True)
    return r * (2.0 - v * r)


def collide(f, g):
    rho, mx, my, mz = moments(f)
    inv = inverse(rho)
    mom = (mx, my, mz)
    u = [m * inv for m in mom]
    y = [(4.5 * W2) * m for m in mom]
    diag = [y[a] * u[a] for a in range(3)]
    o = [(3.0 * W2) * m for m in mom]
    base = W2 * rho - (diag[0] + diag[1] + diag[2]) * (1.0 / 3.0)
    t = [base + d for d in diag]
    post = [None] * 19
    post[0] = f[0] + 12.0 * base
    for a in range(3):
        e, od = t[a] + t[a], o[a] + o[a]
        post[1 + 2 * a] = f[1 + 2 * a] + (e + od)
        post[2 + 2 * a] = f[2 + 2 * a] + (e - od)
    for k, a, b in ((7, 0, 1), (11, 0, 2), (15, 1, 2)):
        e = t[a] + diag[b]
        cross = (y[a] + y[a]) * u[b]
        ep, em = e + cross, e - cross
        op, om = o[a] + o[b], o[a] - o[b]
        post[k] = f[k] + (ep + op)
        post[k + 1] = f[k + 1] + (ep - op)
        post[k + 2] = f[k + 2] + (em + om)
        post[k + 3] = f[k + 3] + (em - om)
    temp = g[0] + (g[1] + g[2]) + (g[3] + g[4]) + (g[5] + g[6])
    eq = (0.125 * OMG) * temp
    eq4 = (0.5 * OMG) * temp
    post.append(LAMG * g[0] + (eq + eq))
    for a in range(3):
        ua = eq4 * u[a]
        post.append(LAMG * g[1 + 2 * a] + (eq + ua))
        post.append(LAMG * g[2 + 2 * a] + (eq - ua))
    return post


def equilibrium(u):
    y = [(4.5 * KAPPA_0) * v for v in u]
    diag = [y[a] * u[a] for a in range(3)]
    o = [(3.0 * KAPPA_0) * v for v in u]
    base = KAPPA_0 - (diag[0] + diag[1] + diag[2]) * (1.0 / 3.0)
    t = [base + d for d in diag]
    f = [None] * 19
    f[0] = 12.0 * base
    for a in range(3):
        e, od = t[a] + t[a], o[a] + o[a]
        f[1 + 2 * a], f[2 + 2 * a] = e + od, e - od
    for k, a, b in ((7, 0, 1), (11, 0, 2), (15, 1, 2)):
        e = t[a] + diag[b]
        cross = (y[a] + y[a]) * u[b]
        ep, em = e + cross, e - cross
        op, om = o[a] + o[b], o[a] - o[b]
        f[k], f[k + 1], f[k + 2], f[k + 3] = ep + op, ep - op, em + om, em - om
    return f


def stream(src, wa, wb, s, xt):
    f = [tile(src, 0, s, xt)]
    g = [tile(src, 19, s, xt)]
    for i in range(1, 19):
        moved = moved_tile(src, i, s, xt)
        open_ = moved < BIG
        f.append(jnp.where(open_, moved, tile(src, OPP[i], s, xt)))
        if i < 7:
            back = tile(src, 19 + OPP[i], s, xt)
            coeff = pl.ds(8 * xt, 8)
            back = wa[i - 1, s, coeff, :] * back + wb[i - 1, s, coeff, :]
            g.append(jnp.where(open_, moved_tile(src, 19 + i, s, xt), back))
    return f, g


def window(zbase, left, own, right, top, bot, temp_out, flow_out, part_out,
           stage, inp, kinds, pops, wa, wb, res):
    height = zbase[1]
    for a in range(5):
        blocks = (left[a], own[a, :, 0:192], own[a, :, 192:384], right[a])
        for q in range(4):
            r0 = 32 * q
            stage[a, r0 : r0 + 8, 0:192] = top[a, :, 192 * q : 192 * q + 192]
            stage[a, r0 + 8 : r0 + 24, 0:192] = blocks[q]
            stage[a, r0 + 24 : r0 + 32, 0:192] = bot[a, :, 192 * q : 192 * q + 192]
        inp[a, 0:16] = stage[a, :, 0:128].T.reshape(16, 8, 128)
        inp[a, 16:24] = stage[a, :, 128:256].T[0:64].reshape(8, 8, 128)

    lane = lax.broadcasted_iota(jnp.int32, (8, 128), 1)
    zin = lane % 32
    mine = (zin >= HALO) & (zin < 32 - HALO) & (lane >= 32) & (lane < 96)
    zpos = zbase[0] + zin.astype(jnp.float32)
    ramp = 0.5 - 0.75 * (zpos + 0.5) / height

    def first(s, carry):
        for xt in range(XT):
            kind = inp[0, s * XT + xt]
            put(kinds, 0, s + 1, xt, kind)
            put(kinds, 1, s + 1, xt, shift_lanes(kind, 1))
            put(kinds, 2, s + 1, xt, shift_lanes(kind, -1))
            fluid = kind == 0.0
            u = [inp[2 + a, s * XT + xt] for a in range(3)]
            temp = ramp + 0.05 * inp[1, s * XT + xt]
            f = equilibrium(u)
            f = [jnp.where(fluid, v, jnp.nan) for v in f]
            eq, eq4 = 0.125 * temp, 0.5 * temp
            f.append(eq + eq)
            for a in range(3):
                ua = eq4 * u[a]
                f.append(eq + ua)
                f.append(eq - ua)
            put_all(pops.at[0], s, xt, f)
        return carry

    lax.fori_loop(0, NS, first, 0, unroll=True)
    copies(pops.at[0])
    for xt in range(XT):
        put(kinds, 0, NS + 1, xt, shift_lanes(tile(kinds, 0, 0, xt), -32))
        put(kinds, 0, 0, xt, shift_lanes(tile(kinds, 0, NS - 1, xt), 32))

    def walls_of(s, carry):
        for xt in range(XT):
            rows = pl.ds(8 * xt, 8)
            for i in range(1, 7):
                c = LAT19[i]
                near = kinds[(0, 1, 2)[c[2]], s + 1 - c[1], pl.ds(8 + 8 * xt - c[0], 8), :]
                hot, cold = near == 2.0, near == 3.0
                wa[i - 1, s, rows, :] = jnp.where(hot | cold, -1.0, 1.0)
                wb[i - 1, s, rows, :] = jnp.where(hot, 0.125, jnp.where(cold, -0.125, 0.0))
        return carry

    lax.fori_loop(0, NS, walls_of, 0, unroll=True)

    def step(k, carry):
        src, dst = pops.at[lax.rem(k + 1, 2)], pops.at[lax.rem(k, 2)]

        def line(s, c):
            for xt in range(XT):
                f, g = stream(src, wa, wb, s, xt)
                put_all(dst, s, xt, collide(f, g))
            return c

        lax.fori_loop(0, NS, line, 0, unroll=4)
        copies(dst)
        return carry

    lax.fori_loop(1, STEPS, step, 0)
    src = pops.at[(STEPS - 1) % 2]

    def last(s, total):
        for xt in range(XT):
            f, g = stream(src, wa, wb, s, xt)
            rho, mx, my, mz = moments(f)
            fluid = f[0] < BIG
            inv = inverse(rho)
            kind = tile(kinds, 0, s, xt)
            walls = jnp.where(kind == 2.0, 0.5, jnp.where(kind == 3.0, -0.5, 0.0))
            temp = g[0] + (g[1] + g[2]) + (g[3] + g[4]) + (g[5] + g[6])
            temp = jnp.where(fluid, temp, walls)
            res[0, s * XT + xt] = temp
            for a, m in enumerate((mx, my, mz)):
                res[1 + a, s * XT + xt] = jnp.where(fluid, m * inv, 0.0)
            heated = fluid & mine & (kinds[0, s, pl.ds(8 + 8 * xt, 8), :] == 2.0)
            total = total + jnp.where(heated, 0.5 - temp, 0.0)
        return total

    total = lax.fori_loop(0, NS, last, jnp.zeros((8, 128), jnp.float32), unroll=True)
    part_out[...] = jnp.full(part_out.shape, jnp.sum(total), jnp.float32)
    for o in range(4):
        one = res[o, 0:16].reshape(128, 128).T
        two = res[o, 16:32].reshape(128, 128).T
        for q in (1, 2):
            rows = slice(32 * q + 8, 32 * q + 24)
            at = 192 * (q - 1)
            val = jnp.concatenate([one[rows], two[rows, 0:64]], axis=1)
            if o == 0:
                temp_out[:, at : at + 192] = val
            else:
                flow_out[o - 1, :, at : at + 192] = val


SCRATCH = [
    pltpu.VMEM((5, 128, 256), jnp.float32),
    pltpu.VMEM((5, NS * XT, 8, 128), jnp.float32),
    pltpu.VMEM((3, NS + 2, ROWS, 128), jnp.float32),
    pltpu.VMEM((2, NCHAN, NS + 2, ROWS, 128), jnp.float32),
    pltpu.VMEM((6, NS, NX, 128), jnp.float32),
    pltpu.VMEM((6, NS, NX, 128), jnp.float32),
    pltpu.VMEM((4, 32, 8, 128), jnp.float32),
]


def all_sum(part, axes, count):
    return jnp.sum(lax.all_to_all(part, axes, 0, 0, tiled=True), axis=0)


def make_body(gz, gy, near, far, n_near, n_far, n_gz, n_gy):
    def body(cell_type, perturb, velocity):
        slab, cells = cell_type.shape
        height = slab * n_gz
        own = jnp.concatenate(
            [
                cell_type.astype(jnp.float32)[None],
                perturb.astype(jnp.float32)[None],
                velocity,
            ]
        )
        rim = HALO * NX
        up = [(i, (i + 1) % n_gy) for i in range(n_gy)]
        down = [((i + 1) % n_gy, i) for i in range(n_gy)]
        left = lax.ppermute(own[:, :, cells - rim :], gy, up)
        right = lax.ppermute(own[:, :, :rim], gy, down)
        wide = jnp.concatenate([left, own, right], axis=2)
        up = [(i, (i + 1) % n_gz) for i in range(n_gz)]
        down = [((i + 1) % n_gz, i) for i in range(n_gz)]
        top = lax.ppermute(wide[:, slab - HALO :], gz, up)
        bot = lax.ppermute(wide[:, :HALO], gz, down)
        zbase = jnp.stack(
            [
                (lax.axis_index(gz) * slab - HALO).astype(jnp.float32),
                jnp.float32(height),
            ]
        )
        vmem = pl.BlockSpec(memory_space=pltpu.VMEM)
        f32 = jnp.float32
        temp, flow, part = pl.pallas_call(
            window,
            in_specs=[pl.BlockSpec(memory_space=pltpu.SMEM)] + [vmem] * 5,
            out_specs=[vmem] * 3,
            out_shape=[
                jax.ShapeDtypeStruct((slab, cells), f32),
                jax.ShapeDtypeStruct((3, slab, cells), f32),
                jax.ShapeDtypeStruct((n_near, 128), f32),
            ],
            scratch_shapes=SCRATCH,
            compiler_params=pltpu.CompilerParams(vmem_limit_bytes=40 * 1024 * 1024),
            name="lattice_window",
        )(zbase, left, own, right, top, bot)
        line = all_sum(part, near, n_near)
        line = all_sum(jnp.broadcast_to(line, (n_far, 128)), far, n_far)
        return temp, flow, line[0] * (2.0 / (NX * height))

    return body


def solution(mesh):
    n_gz, n_gy = mesh.shape["gz"], mesh.shape["gy"]
    z = n_gz // 4
    fine = Mesh(
        np.asarray(mesh.devices).reshape(2, z, 2, n_gy),
        ("yl", "z", "core", "gy"),
    )
    gz = ("yl", "z", "core")
    near = ("yl", "core", "gy")
    body = make_body(gz, "gy", near, "z", 4 * n_gy, z, n_gz, n_gy)
    return jax.shard_map(
        body,
        mesh=fine,
        in_specs=(P(gz, "gy"), P(gz, "gy"), P(None, gz, "gy")),
        out_specs=(P(gz, "gy"), P(None, gz, "gy"), P()),
        check_vma=False,
    )
```

```python
import numpy as np

import jax
import jax.numpy as jnp
from jax import lax
from jax.experimental import pallas as pl
from jax.experimental.pallas import tpu as pltpu
from jax.sharding import Mesh, PartitionSpec as P

NX = 24
STEPS = 8
HALO = STEPS
TAU_F = 0.52
TAU_G = 0.5376
LAT19 = [
    (0, 0, 0),
    (1, 0, 0),
    (-1, 0, 0),
    (0, 1, 0),
    (0, -1, 0),
    (0, 0, 1),
    (0, 0, -1),
    (1, 1, 0),
    (-1, -1, 0),
    (1, -1, 0),
    (-1, 1, 0),
    (1, 0, 1),
    (-1, 0, -1),
    (1, 0, -1),
    (-1, 0, 1),
    (0, 1, 1),
    (0, -1, -1),
    (0, 1, -1),
    (0, -1, 1),
]
WGT19 = [1.0 / 3.0] + [1.0 / 18.0] * 6 + [1.0 / 36.0] * 12
LAT7 = LAT19[:7]
WGT7 = [0.25] + [0.125] * 6
OPP = [LAT19.index(tuple(-v for v in c)) for c in LAT19]

KAPPA = -1.0 / (1.0 - TAU_F)
W2 = KAPPA / 36.0
KAPPA_0 = 1.0 / 36.0 / (1.0 - 1.0 / TAU_F)
OMG = 1.0 / TAU_G
LAMG = 1.0 - OMG
BIG = 1e30

NS = 8
XT = NX // 8
ROWS = 40


COPY = list(range(26))
for _i in range(1, 19):
    if LAT19[_i][2]:
        COPY[_i] = 26 + sum(1 for c in COPY if c >= 26)
for _i in range(1, 7):
    if LAT19[_i][2]:
        COPY[19 + _i] = 26 + sum(1 for c in COPY if c >= 26)
NCHAN = 26 + sum(1 for c in COPY if c >= 26)


def shift_lanes(v, by):
    return pltpu.roll(v, by % 128, axis=1)


def velocity_of(chan):
    return LAT19[chan] if chan < 19 else LAT19[chan - 19]


def put(ref, chan, slot, xt, v):
    ref[chan, slot, pl.ds(8 + 8 * xt, 8), :] = v


def tile(ref, chan, s, xt):
    return ref[chan, s + 1, pl.ds(8 + 8 * xt, 8), :]


def moved_tile(ref, chan, s, xt):
    c = velocity_of(chan)
    return ref[COPY[chan], s + 1 - c[1], pl.ds(8 + 8 * xt - c[0], 8), :]


def put_all(ref, s, xt, post):
    for chan, v in enumerate(post):
        put(ref, chan, s + 1, xt, v)


def copies(ref):
    def roll_line(s, carry):
        for xt in range(XT):
            for chan in range(26):
                c = velocity_of(chan)
                if c[2]:
                    put(ref, COPY[chan], s + 1, xt, shift_lanes(tile(ref, chan, s, xt), c[2]))
        return carry

    for xt in range(XT):
        for chan in range(26):
            c = velocity_of(chan)
            if c[1] > 0:
                put(ref, COPY[chan], 0, xt, shift_lanes(tile(ref, chan, NS - 1, xt), c[2] + 32))
            if c[1] < 0:
                put(ref, COPY[chan], NS + 1, xt, shift_lanes(tile(ref, chan, 0, xt), c[2] - 32))
    lax.fori_loop(0, NS, roll_line, 0, unroll=True)


def moments(f):
    quad = []
    for k in (7, 11, 15):
        p, m = f[k] + f[k + 2], f[k + 1] + f[k + 3]
        quad.append((p + m, p - m, (f[k] - f[k + 2]) - (f[k + 1] - f[k + 3])))
    rho = f[0] + (f[1] + f[2]) + (f[3] + f[4]) + (f[5] + f[6])
    rho = rho + quad[0][0] + quad[1][0] + quad[2][0]
    mx = (f[1] - f[2]) + quad[0][1] + quad[1][1]
    my = (f[3] - f[4]) + quad[0][2] + quad[2][1]
    mz = (f[5] - f[6]) + quad[1][2] + quad[2][2]
    return rho, mx, my, mz


def inverse(v):
    r = pl.reciprocal(v, approx=True)
    return r * (2.0 - v * r)


def collide(f, g):
    rho, mx, my, mz = moments(f)
    inv = inverse(rho)
    mom = (mx, my, mz)
    u = [m * inv for m in mom]
    y = [(4.5 * W2) * m for m in mom]
    diag = [y[a] * u[a] for a in range(3)]
    o = [(3.0 * W2) * m for m in mom]
    base = W2 * rho - (diag[0] + diag[1] + diag[2]) * (1.0 / 3.0)
    t = [base + d for d in diag]
    post = [None] * 19
    post[0] = f[0] + 12.0 * base
    for a in range(3):
        e, od = t[a] + t[a], o[a] + o[a]
        post[1 + 2 * a] = f[1 + 2 * a] + (e + od)
        post[2 + 2 * a] = f[2 + 2 * a] + (e - od)
    for k, a, b in ((7, 0, 1), (11, 0, 2), (15, 1, 2)):
        e = t[a] + diag[b]
        cross = (y[a] + y[a]) * u[b]
        ep, em = e + cross, e - cross
        op, om = o[a] + o[b], o[a] - o[b]
        post[k] = f[k] + (ep + op)
        post[k + 1] = f[k + 1] + (ep - op)
        post[k + 2] = f[k + 2] + (em + om)
        post[k + 3] = f[k + 3] + (em - om)
    temp = g[0] + (g[1] + g[2]) + (g[3] + g[4]) + (g[5] + g[6])
    eq = (0.125 * OMG) * temp
    eq4 = (0.5 * OMG) * temp
    post.append(LAMG * g[0] + (eq + eq))
    for a in range(3):
        ua = eq4 * u[a]
        post.append(LAMG * g[1 + 2 * a] + (eq + ua))
        post.append(LAMG * g[2 + 2 * a] + (eq - ua))
    return post


def equilibrium(u):
    y = [(4.5 * KAPPA_0) * v for v in u]
    diag = [y[a] * u[a] for a in range(3)]
    o = [(3.0 * KAPPA_0) * v for v in u]
    base = KAPPA_0 - (diag[0] + diag[1] + diag[2]) * (1.0 / 3.0)
    t = [base + d for d in diag]
    f = [None] * 19
    f[0] = 12.0 * base
    for a in range(3):
        e, od = t[a] + t[a], o[a] + o[a]
        f[1 + 2 * a], f[2 + 2 * a] = e + od, e - od
    for k, a, b in ((7, 0, 1), (11, 0, 2), (15, 1, 2)):
        e = t[a] + diag[b]
        cross = (y[a] + y[a]) * u[b]
        ep, em = e + cross, e - cross
        op, om = o[a] + o[b], o[a] - o[b]
        f[k], f[k + 1], f[k + 2], f[k + 3] = ep + op, ep - op, em + om, em - om
    return f


def stream(src, wa, wb, s, xt):
    f = [tile(src, 0, s, xt)]
    g = [tile(src, 19, s, xt)]
    for i in range(1, 19):
        moved = moved_tile(src, i, s, xt)
        open_ = moved < BIG
        f.append(jnp.where(open_, moved, tile(src, OPP[i], s, xt)))
        if i < 7:
            back = tile(src, 19 + OPP[i], s, xt)
            coeff = pl.ds(8 * xt, 8)
            back = wa[i - 1, s, coeff, :] * back + wb[i - 1, s, coeff, :]
            g.append(jnp.where(open_, moved_tile(src, 19 + i, s, xt), back))
    return f, g


def window(zbase, left, own, right, top, bot, temp_out, flow_out, part_out,
           stage, inp, kinds, pops, wa, wb, res):
    height = zbase[1]
    for a in range(5):
        blocks = (left[a], own[a, :, 0:192], own[a, :, 192:384], right[a])
        for q in range(4):
            r0 = 32 * q
            stage[a, r0 : r0 + 8, 0:192] = top[a, :, 192 * q : 192 * q + 192]
            stage[a, r0 + 8 : r0 + 24, 0:192] = blocks[q]
            stage[a, r0 + 24 : r0 + 32, 0:192] = bot[a, :, 192 * q : 192 * q + 192]
        inp[a, 0:16] = stage[a, :, 0:128].T.reshape(16, 8, 128)
        inp[a, 16:24] = stage[a, :, 128:256].T[0:64].reshape(8, 8, 128)

    lane = lax.broadcasted_iota(jnp.int32, (8, 128), 1)
    zin = lane % 32
    mine = (zin >= HALO) & (zin < 32 - HALO) & (lane >= 32) & (lane < 96)
    zpos = zbase[0] + zin.astype(jnp.float32)
    ramp = 0.5 - 0.75 * (zpos + 0.5) / height

    def first(s, carry):
        for xt in range(XT):
            kind = inp[0, s * XT + xt]
            put(kinds, 0, s + 1, xt, kind)
            put(kinds, 1, s + 1, xt, shift_lanes(kind, 1))
            put(kinds, 2, s + 1, xt, shift_lanes(kind, -1))
            fluid = kind == 0.0
            u = [inp[2 + a, s * XT + xt] for a in range(3)]
            temp = ramp + 0.05 * inp[1, s * XT + xt]
            f = equilibrium(u)
            f = [jnp.where(fluid, v, jnp.nan) for v in f]
            eq, eq4 = 0.125 * temp, 0.5 * temp
            f.append(eq + eq)
            for a in range(3):
                ua = eq4 * u[a]
                f.append(eq + ua)
                f.append(eq - ua)
            put_all(pops.at[0], s, xt, f)
        return carry

    lax.fori_loop(0, NS, first, 0, unroll=True)
    copies(pops.at[0])
    for xt in range(XT):
        put(kinds, 0, NS + 1, xt, shift_lanes(tile(kinds, 0, 0, xt), -32))
        put(kinds, 0, 0, xt, shift_lanes(tile(kinds, 0, NS - 1, xt), 32))

    def walls_of(s, carry):
        for xt in range(XT):
            rows = pl.ds(8 * xt, 8)
            for i in range(1, 7):
                c = LAT19[i]
                near = kinds[(0, 1, 2)[c[2]], s + 1 - c[1], pl.ds(8 + 8 * xt - c[0], 8), :]
                hot, cold = near == 2.0, near == 3.0
                wa[i - 1, s, rows, :] = jnp.where(hot | cold, -1.0, 1.0)
                wb[i - 1, s, rows, :] = jnp.where(hot, 0.125, jnp.where(cold, -0.125, 0.0))
        return carry

    lax.fori_loop(0, NS, walls_of, 0, unroll=True)

    def step(k, carry):
        src, dst = pops.at[lax.rem(k + 1, 2)], pops.at[lax.rem(k, 2)]

        def line(s, c):
            for xt in range(XT):
                f, g = stream(src, wa, wb, s, xt)
                put_all(dst, s, xt, collide(f, g))
            return c

        lax.fori_loop(0, NS, line, 0, unroll=4)
        copies(dst)
        return carry

    lax.fori_loop(1, STEPS, step, 0)
    src = pops.at[(STEPS - 1) % 2]

    def last(s, total):
        for xt in range(XT):
            f, g = stream(src, wa, wb, s, xt)
            rho, mx, my, mz = moments(f)
            fluid = f[0] < BIG
            inv = inverse(rho)
            kind = tile(kinds, 0, s, xt)
            walls = jnp.where(kind == 2.0, 0.5, jnp.where(kind == 3.0, -0.5, 0.0))
            temp = g[0] + (g[1] + g[2]) + (g[3] + g[4]) + (g[5] + g[6])
            temp = jnp.where(fluid, temp, walls)
            res[0, s * XT + xt] = temp
            for a, m in enumerate((mx, my, mz)):
                res[1 + a, s * XT + xt] = jnp.where(fluid, m * inv, 0.0)
            heated = fluid & mine & (kinds[0, s, pl.ds(8 + 8 * xt, 8), :] == 2.0)
            total = total + jnp.where(heated, 0.5 - temp, 0.0)
        return total

    total = lax.fori_loop(0, NS, last, jnp.zeros((8, 128), jnp.float32), unroll=True)
    part_out[...] = jnp.full(part_out.shape, jnp.sum(total), jnp.float32)
    for o in range(4):
        one = res[o, 0:16].reshape(128, 128).T
        two = res[o, 16:32].reshape(128, 128).T
        for q in (1, 2):
            rows = slice(32 * q + 8, 32 * q + 24)
            at = 192 * (q - 1)
            val = jnp.concatenate([one[rows], two[rows, 0:64]], axis=1)
            if o == 0:
                temp_out[:, at : at + 192] = val
            else:
                flow_out[o - 1, :, at : at + 192] = val


SCRATCH = [
    pltpu.VMEM((5, 128, 256), jnp.float32),
    pltpu.VMEM((5, NS * XT, 8, 128), jnp.float32),
    pltpu.VMEM((3, NS + 2, ROWS, 128), jnp.float32),
    pltpu.VMEM((2, NCHAN, NS + 2, ROWS, 128), jnp.float32),
    pltpu.VMEM((6, NS, NX, 128), jnp.float32),
    pltpu.VMEM((6, NS, NX, 128), jnp.float32),
    pltpu.VMEM((4, 32, 8, 128), jnp.float32),
]


def all_sum(part, axes, count, first):
    order = [[(i + first) % count for i in range(count)]]
    parts = lax.all_to_all(part, axes, 0, 0, tiled=True, axis_index_groups=order)
    return jnp.sum(parts, axis=0)


def make_body(gz, gy, near, far, n_near, n_far, n_gz, n_gy):
    def body(cell_type, perturb, velocity):
        slab, cells = cell_type.shape
        height = slab * n_gz
        own = jnp.concatenate(
            [
                cell_type.astype(jnp.float32)[None],
                perturb.astype(jnp.float32)[None],
                velocity,
            ]
        )
        rim = HALO * NX
        up = [(i, (i + 1) % n_gy) for i in range(n_gy)]
        down = [((i + 1) % n_gy, i) for i in range(n_gy)]
        left = lax.ppermute(own[:, :, cells - rim :], gy, up)
        right = lax.ppermute(own[:, :, :rim], gy, down)
        wide = jnp.concatenate([left, own, right], axis=2)
        up = [(i, (i + 1) % n_gz) for i in range(n_gz)]
        down = [((i + 1) % n_gz, i) for i in range(n_gz)]
        top = lax.ppermute(wide[:, slab - HALO :], gz, up)
        bot = lax.ppermute(wide[:, :HALO], gz, down)
        zbase = jnp.stack(
            [
                (lax.axis_index(gz) * slab - HALO).astype(jnp.float32),
                jnp.float32(height),
            ]
        )
        vmem = pl.BlockSpec(memory_space=pltpu.VMEM)
        f32 = jnp.float32
        temp, flow, part = pl.pallas_call(
            window,
            in_specs=[pl.BlockSpec(memory_space=pltpu.SMEM)] + [vmem] * 5,
            out_specs=[vmem] * 3,
            out_shape=[
                jax.ShapeDtypeStruct((slab, cells), f32),
                jax.ShapeDtypeStruct((3, slab, cells), f32),
                jax.ShapeDtypeStruct((n_near, 128), f32),
            ],
            scratch_shapes=SCRATCH,
            compiler_params=pltpu.CompilerParams(vmem_limit_bytes=40 * 1024 * 1024),
            name="lattice_window",
        )(zbase, left, own, right, top, bot)
        line = all_sum(part, near, n_near, n_gy + 5 * n_gy // 8)
        line = all_sum(jnp.broadcast_to(line, (n_far, 128)), far, n_far, 9 * n_far // 16)
        return temp, flow, line[0] * (2.0 / (NX * height))

    return body


def solution(mesh):
    n_gz, n_gy = mesh.shape["gz"], mesh.shape["gy"]
    z = n_gz // 4
    fine = Mesh(
        np.asarray(mesh.devices).reshape(2, z, 2, n_gy),
        ("yl", "z", "core", "gy"),
    )
    gz = ("yl", "z", "core")
    near = ("yl", "core", "gy")
    body = make_body(gz, "gy", near, "z", 4 * n_gy, z, n_gz, n_gy)
    return jax.shard_map(
        body,
        mesh=fine,
        in_specs=(P(gz, "gy"), P(gz, "gy"), P(None, gz, "gy")),
        out_specs=(P(gz, "gy"), P(None, gz, "gy"), P()),
        check_vma=False,
    )
```

```python
import numpy as np

import jax
import jax.numpy as jnp
from jax import lax
from jax.experimental import pallas as pl
from jax.experimental.pallas import tpu as pltpu
from jax.sharding import Mesh, PartitionSpec as P

NX = 24
STEPS = 8
HALO = STEPS
TAU_F = 0.52
TAU_G = 0.5376
LAT19 = [
    (0, 0, 0),
    (1, 0, 0),
    (-1, 0, 0),
    (0, 1, 0),
    (0, -1, 0),
    (0, 0, 1),
    (0, 0, -1),
    (1, 1, 0),
    (-1, -1, 0),
    (1, -1, 0),
    (-1, 1, 0),
    (1, 0, 1),
    (-1, 0, -1),
    (1, 0, -1),
    (-1, 0, 1),
    (0, 1, 1),
    (0, -1, -1),
    (0, 1, -1),
    (0, -1, 1),
]
WGT19 = [1.0 / 3.0] + [1.0 / 18.0] * 6 + [1.0 / 36.0] * 12
LAT7 = LAT19[:7]
WGT7 = [0.25] + [0.125] * 6
OPP = [LAT19.index(tuple(-v for v in c)) for c in LAT19]

KAPPA = -1.0 / (1.0 - TAU_F)
W2 = KAPPA / 36.0
KAPPA_0 = 1.0 / 36.0 / (1.0 - 1.0 / TAU_F)
OMG = 1.0 / TAU_G
LAMG = 1.0 - OMG
BIG = 1e30

NS = 8
XT = NX // 8
ROWS = 40


COPY = list(range(26))
for _i in range(1, 19):
    if LAT19[_i][2]:
        COPY[_i] = 26 + sum(1 for c in COPY if c >= 26)
for _i in range(1, 7):
    if LAT19[_i][2]:
        COPY[19 + _i] = 26 + sum(1 for c in COPY if c >= 26)
NCHAN = 26 + sum(1 for c in COPY if c >= 26)


def shift_lanes(v, by):
    return pltpu.roll(v, by % 128, axis=1)


def velocity_of(chan):
    return LAT19[chan] if chan < 19 else LAT19[chan - 19]


def put(ref, chan, slot, xt, v):
    ref[chan, slot, pl.ds(8 + 8 * xt, 8), :] = v


def tile(ref, chan, s, xt):
    return ref[chan, s + 1, pl.ds(8 + 8 * xt, 8), :]


def moved_tile(ref, chan, s, xt):
    c = velocity_of(chan)
    return ref[COPY[chan], s + 1 - c[1], pl.ds(8 + 8 * xt - c[0], 8), :]


def put_all(ref, s, xt, post):
    for chan, v in enumerate(post):
        put(ref, chan, s + 1, xt, v)


def copies(ref):
    def roll_line(s, carry):
        for xt in range(XT):
            for chan in range(26):
                c = velocity_of(chan)
                if c[2]:
                    put(ref, COPY[chan], s + 1, xt, shift_lanes(tile(ref, chan, s, xt), c[2]))
        return carry

    for xt in range(XT):
        for chan in range(26):
            c = velocity_of(chan)
            if c[1] > 0:
                put(ref, COPY[chan], 0, xt, shift_lanes(tile(ref, chan, NS - 1, xt), c[2] + 32))
            if c[1] < 0:
                put(ref, COPY[chan], NS + 1, xt, shift_lanes(tile(ref, chan, 0, xt), c[2] - 32))
    lax.fori_loop(0, NS, roll_line, 0, unroll=True)


def moments(f):
    quad = []
    for k in (7, 11, 15):
        p, m = f[k] + f[k + 2], f[k + 1] + f[k + 3]
        quad.append((p + m, p - m, (f[k] - f[k + 2]) - (f[k + 1] - f[k + 3])))
    rho = f[0] + (f[1] + f[2]) + (f[3] + f[4]) + (f[5] + f[6])
    rho = rho + quad[0][0] + quad[1][0] + quad[2][0]
    mx = (f[1] - f[2]) + quad[0][1] + quad[1][1]
    my = (f[3] - f[4]) + quad[0][2] + quad[2][1]
    mz = (f[5] - f[6]) + quad[1][2] + quad[2][2]
    return rho, mx, my, mz


def inverse(v):
    r = pl.reciprocal(v, approx=True)
    return r * (2.0 - v * r)


def collide(f, g):
    rho, mx, my, mz = moments(f)
    inv = inverse(rho)
    mom = (mx, my, mz)
    u = [m * inv for m in mom]
    y = [(4.5 * W2) * m for m in mom]
    diag = [y[a] * u[a] for a in range(3)]
    o = [(3.0 * W2) * m for m in mom]
    base = W2 * rho - (diag[0] + diag[1] + diag[2]) * (1.0 / 3.0)
    t = [base + d for d in diag]
    post = [None] * 19
    post[0] = f[0] + 12.0 * base
    for a in range(3):
        e, od = t[a] + t[a], o[a] + o[a]
        post[1 + 2 * a] = f[1 + 2 * a] + (e + od)
        post[2 + 2 * a] = f[2 + 2 * a] + (e - od)
    for k, a, b in ((7, 0, 1), (11, 0, 2), (15, 1, 2)):
        e = t[a] + diag[b]
        cross = (y[a] + y[a]) * u[b]
        ep, em = e + cross, e - cross
        op, om = o[a] + o[b], o[a] - o[b]
        post[k] = f[k] + (ep + op)
        post[k + 1] = f[k + 1] + (ep - op)
        post[k + 2] = f[k + 2] + (em + om)
        post[k + 3] = f[k + 3] + (em - om)
    temp = g[0] + (g[1] + g[2]) + (g[3] + g[4]) + (g[5] + g[6])
    eq = (0.125 * OMG) * temp
    eq4 = (0.5 * OMG) * temp
    post.append(LAMG * g[0] + (eq + eq))
    for a in range(3):
        ua = eq4 * u[a]
        post.append(LAMG * g[1 + 2 * a] + (eq + ua))
        post.append(LAMG * g[2 + 2 * a] + (eq - ua))
    return post


def equilibrium(u):
    y = [(4.5 * KAPPA_0) * v for v in u]
    diag = [y[a] * u[a] for a in range(3)]
    o = [(3.0 * KAPPA_0) * v for v in u]
    base = KAPPA_0 - (diag[0] + diag[1] + diag[2]) * (1.0 / 3.0)
    t = [base + d for d in diag]
    f = [None] * 19
    f[0] = 12.0 * base
    for a in range(3):
        e, od = t[a] + t[a], o[a] + o[a]
        f[1 + 2 * a], f[2 + 2 * a] = e + od, e - od
    for k, a, b in ((7, 0, 1), (11, 0, 2), (15, 1, 2)):
        e = t[a] + diag[b]
        cross = (y[a] + y[a]) * u[b]
        ep, em = e + cross, e - cross
        op, om = o[a] + o[b], o[a] - o[b]
        f[k], f[k + 1], f[k + 2], f[k + 3] = ep + op, ep - op, em + om, em - om
    return f


def stream(src, wa, wb, s, xt):
    f = [tile(src, 0, s, xt)]
    g = [tile(src, 19, s, xt)]
    for i in range(1, 19):
        moved = moved_tile(src, i, s, xt)
        open_ = moved < BIG
        f.append(jnp.where(open_, moved, tile(src, OPP[i], s, xt)))
        if i < 7:
            back = tile(src, 19 + OPP[i], s, xt)
            c = LAT19[i]
            near = (c[2] % 3, s + 1 - c[1], pl.ds(8 + 8 * xt - c[0], 8))
            back = wa[near] * back + wb[near]
            g.append(jnp.where(open_, moved_tile(src, 19 + i, s, xt), back))
    return f, g


def window(zbase, left, own, right, top, bot, temp_out, flow_out, part_out,
           stage, inp, pops, wa, wb, res):
    height = zbase[1]
    for a in range(5):
        p, half = 5 + a // 2, 64 * (a % 2)
        parts = (
            (8, 16, [own[3 * a + j] for j in range(3)], left, right),
            (0, 8, [top[3 * a + j] for j in range(3)], top.at[15:23], top.at[23:31]),
            (24, 8, [bot[3 * a + j] for j in range(3)], bot.at[15:23], bot.at[23:31]),
        )
        for z0, n, mid, lo, hi in parts:
            low = ((0, lo[a]), (3, hi[a]), (1, mid[0]), (2, mid[2]))
            ends = (lo[p, :, half : half + 64], hi[p, :, half : half + 64])
            for q, v in low:
                r = slice(32 * q + z0, 32 * q + z0 + n)
                if q % 2:
                    stage[a, r, 0:128] = v
                    stage[a, r, 128:192] = ends[1] if q == 3 else mid[1][:, 0:64]
                else:
                    stage[a, r, 0:64] = mid[1][:, 64:128] if q else ends[0]
                    stage[a, r, 64:192] = v
        inp[a, 0:16] = stage[a, :, 0:128].T.reshape(16, 8, 128)
        inp[a, 16:24] = stage[a, :, 128:256].T[0:64].reshape(8, 8, 128)

    lane = lax.broadcasted_iota(jnp.int32, (8, 128), 1)
    zin = lane % 32
    mine = (zin >= HALO) & (zin < 32 - HALO) & (lane >= 32) & (lane < 96)
    zpos = zbase[0] + zin.astype(jnp.float32)
    ramp = 0.5 - 0.75 * (zpos + 0.5) / height

    def first(s):
        for xt in range(XT):
            kind = inp[0, s * XT + xt]
            hot, cold = kind == 2.0, kind == 3.0
            sign = jnp.where(hot | cold, -1.0, 1.0)
            gain = jnp.where(hot, 0.125, jnp.where(cold, -0.125, 0.0))
            for ref, v in ((wa, sign), (wb, gain)):
                for chan in range(3):
                    put(ref, chan, s + 1, xt, shift_lanes(v, (0, 1, -1)[chan]) if chan else v)
                if s == 0:
                    put(ref, 0, NS + 1, xt, shift_lanes(v, -32))
                if s == NS - 1:
                    put(ref, 0, 0, xt, shift_lanes(v, 32))
            fluid = kind == 0.0
            u = [inp[2 + a, s * XT + xt] for a in range(3)]
            temp = ramp + 0.05 * inp[1, s * XT + xt]
            f = equilibrium(u)
            f = [jnp.where(fluid, v, jnp.nan) for v in f]
            eq, eq4 = 0.125 * temp, 0.5 * temp
            f.append(eq + eq)
            for a in range(3):
                ua = eq4 * u[a]
                f.append(eq + ua)
                f.append(eq - ua)
            put_all(pops.at[0], s, xt, f)

    for s in range(NS):
        first(s)
    copies(pops.at[0])

    def step(k, carry):
        src, dst = pops.at[lax.rem(k + 1, 2)], pops.at[lax.rem(k, 2)]

        def line(s, c):
            for xt in range(XT):
                f, g = stream(src, wa, wb, s, xt)
                put_all(dst, s, xt, collide(f, g))
            return c

        lax.fori_loop(0, NS, line, 0, unroll=4)
        copies(dst)
        return carry

    lax.fori_loop(1, STEPS, step, 0)
    src = pops.at[(STEPS - 1) % 2]

    def last(s, total):
        for xt in range(XT):
            f, g = stream(src, wa, wb, s, xt)
            rho, mx, my, mz = moments(f)
            fluid = f[0] < BIG
            inv = inverse(rho)
            kind = inp[0, s * XT + xt]
            walls = jnp.where(kind == 2.0, 0.5, jnp.where(kind == 3.0, -0.5, 0.0))
            temp = g[0] + (g[1] + g[2]) + (g[3] + g[4]) + (g[5] + g[6])
            temp = jnp.where(fluid, temp, walls)
            res[0, s * XT + xt] = temp
            for a, m in enumerate((mx, my, mz)):
                res[1 + a, s * XT + xt] = jnp.where(fluid, m * inv, 0.0)
            heated = fluid & mine & (wb[0, s, pl.ds(8 + 8 * xt, 8), :] == 0.125)
            total = total + jnp.where(heated, 0.5 - temp, 0.0)
        return total

    total = lax.fori_loop(0, NS, last, jnp.zeros((8, 128), jnp.float32), unroll=True)
    part_out[...] = jnp.full(part_out.shape, jnp.sum(total), jnp.float32)
    for o in range(4):
        one = res[o, 0:16].reshape(128, 128).T
        two = res[o, 16:32].reshape(128, 128).T
        for q in (1, 2):
            rows = slice(32 * q + 8, 32 * q + 24)
            at = 192 * (q - 1)
            val = jnp.concatenate([one[rows], two[rows, 0:64]], axis=1)
            if o == 0:
                temp_out[:, at : at + 192] = val
            else:
                flow_out[o - 1, :, at : at + 192] = val


SCRATCH = [
    pltpu.VMEM((5, 128, 256), jnp.float32),
    pltpu.VMEM((5, NS * XT, 8, 128), jnp.float32),
    pltpu.VMEM((2, NCHAN, NS + 2, ROWS, 128), jnp.float32),
    pltpu.VMEM((3, NS + 2, ROWS, 128), jnp.float32),
    pltpu.VMEM((3, NS + 2, ROWS, 128), jnp.float32),
    pltpu.VMEM((4, 32, 8, 128), jnp.float32),
]


def pack_sides(cell_type, perturb, velocity, own, low, high, kind, noise, speed, sems):
    moves = [
        pltpu.make_async_copy(src, dst, sems.at[i])
        for i, (src, dst) in enumerate(((cell_type, kind), (perturb, noise), (velocity, speed)))
    ]
    for move in moves:
        move.start()
    for move in moves:
        move.wait()
    fields = [kind[...].astype(jnp.float32), noise[...].astype(jnp.float32)]
    fields += [speed[a] for a in range(3)]
    for a, f in enumerate(fields):
        for j in range(3):
            own[3 * a + j] = f[:, 128 * j : 128 * j + 128]
        low[a] = f[:, 0:128]
        high[a] = f[:, 256:384]
    for p in range(3):
        one, two = fields[2 * p], fields[min(2 * p + 1, 4)]
        low[5 + p] = jnp.concatenate([one[:, 128:192], two[:, 128:192]], axis=1)
        high[5 + p] = jnp.concatenate([one[:, 192:256], two[:, 192:256]], axis=1)


def pack_ends(own, left, right, first, final):
    rows = own.shape[1]
    for ref, at in ((own, 0), (left, 15), (right, 23)):
        n = ref.shape[0]
        first[at : at + n] = ref[:, 0:HALO]
        final[at : at + n] = ref[:, rows - HALO : rows]


def all_sum(part, axes, count, first):
    order = [[(i + first) % count for i in range(count)]]
    parts = lax.all_to_all(part, axes, 0, 0, tiled=True, axis_index_groups=order)
    return jnp.sum(parts, axis=0)


def make_body(gz, gy, near, far, n_near, n_far, n_gz, n_gy):
    def body(cell_type, perturb, velocity):
        slab, cells = cell_type.shape
        height = slab * n_gz
        vmem = pl.BlockSpec(memory_space=pltpu.VMEM)
        f32 = jnp.float32

        def tiles(n, rows):
            return jax.ShapeDtypeStruct((n, rows, 128), f32)

        own, low, high = pl.pallas_call(
            pack_sides,
            in_specs=[pl.BlockSpec(memory_space=pl.ANY)] * 3,
            out_specs=[vmem] * 3,
            out_shape=[tiles(15, slab), tiles(8, slab), tiles(8, slab)],
            scratch_shapes=[
                pltpu.VMEM((slab, cells), jnp.int32),
                pltpu.VMEM((slab, cells), jnp.int32),
                pltpu.VMEM((3, slab, cells), f32),
                pltpu.SemaphoreType.DMA((3,)),
            ],
            name="pack_sides",
        )(cell_type, perturb, velocity)
        up = [(i, (i + 1) % n_gy) for i in range(n_gy)]
        down = [((i + 1) % n_gy, i) for i in range(n_gy)]
        left = lax.ppermute(high, gy, up)
        right = lax.ppermute(low, gy, down)
        first, final = pl.pallas_call(
            pack_ends,
            in_specs=[vmem] * 3,
            out_specs=[vmem] * 2,
            out_shape=[tiles(31, HALO), tiles(31, HALO)],
            name="pack_ends",
        )(own, left, right)
        up = [(i, (i + 1) % n_gz) for i in range(n_gz)]
        down = [((i + 1) % n_gz, i) for i in range(n_gz)]
        top = lax.ppermute(final, gz, up)
        bot = lax.ppermute(first, gz, down)
        zbase = jnp.stack(
            [
                (lax.axis_index(gz) * slab - HALO).astype(jnp.float32),
                jnp.float32(height),
            ]
        )
        temp, flow, part = pl.pallas_call(
            window,
            in_specs=[pl.BlockSpec(memory_space=pltpu.SMEM)] + [vmem] * 5,
            out_specs=[vmem] * 3,
            out_shape=[
                jax.ShapeDtypeStruct((slab, cells), f32),
                jax.ShapeDtypeStruct((3, slab, cells), f32),
                jax.ShapeDtypeStruct((n_near, 128), f32),
            ],
            scratch_shapes=SCRATCH,
            compiler_params=pltpu.CompilerParams(vmem_limit_bytes=40 * 1024 * 1024),
            name="lattice_window",
        )(zbase, left, own, right, top, bot)
        line = all_sum(part, near, n_near, n_gy + 5 * n_gy // 8)
        line = all_sum(jnp.broadcast_to(line, (n_far, 128)), far, n_far, 9 * n_far // 16)
        return temp, flow, line[0] * (2.0 / (NX * height))

    return body


def solution(mesh):
    n_gz, n_gy = mesh.shape["gz"], mesh.shape["gy"]
    z = n_gz // 4
    fine = Mesh(
        np.asarray(mesh.devices).reshape(2, z, 2, n_gy),
        ("yl", "z", "core", "gy"),
    )
    gz = ("yl", "z", "core")
    near = ("yl", "core", "gy")
    body = make_body(gz, "gy", near, "z", 4 * n_gy, z, n_gz, n_gy)
    return jax.shard_map(
        body,
        mesh=fine,
        in_specs=(P(gz, "gy"), P(gz, "gy"), P(None, gz, "gy")),
        out_specs=(P(gz, "gy"), P(None, gz, "gy"), P()),
        check_vma=False,
    )
```

```python
import numpy as np

import jax
import jax.numpy as jnp
from jax import lax
from jax.experimental import pallas as pl
from jax.experimental.pallas import tpu as pltpu
from jax.sharding import Mesh, PartitionSpec as P

NX = 24
STEPS = 8
HALO = STEPS
TAU_F = 0.52
TAU_G = 0.5376
LAT19 = [
    (0, 0, 0),
    (1, 0, 0),
    (-1, 0, 0),
    (0, 1, 0),
    (0, -1, 0),
    (0, 0, 1),
    (0, 0, -1),
    (1, 1, 0),
    (-1, -1, 0),
    (1, -1, 0),
    (-1, 1, 0),
    (1, 0, 1),
    (-1, 0, -1),
    (1, 0, -1),
    (-1, 0, 1),
    (0, 1, 1),
    (0, -1, -1),
    (0, 1, -1),
    (0, -1, 1),
]
WGT19 = [1.0 / 3.0] + [1.0 / 18.0] * 6 + [1.0 / 36.0] * 12
LAT7 = LAT19[:7]
WGT7 = [0.25] + [0.125] * 6
OPP = [LAT19.index(tuple(-v for v in c)) for c in LAT19]

KAPPA = -1.0 / (1.0 - TAU_F)
W2 = KAPPA / 36.0
KAPPA_0 = 1.0 / 36.0 / (1.0 - 1.0 / TAU_F)
OMG = 1.0 / TAU_G
LAMG = 1.0 - OMG
BIG = 1e30

NS = 8
XT = NX // 8
ROWS = 40


COPY = list(range(26))
for _i in range(1, 19):
    if LAT19[_i][2]:
        COPY[_i] = 26 + sum(1 for c in COPY if c >= 26)
for _i in range(1, 7):
    if LAT19[_i][2]:
        COPY[19 + _i] = 26 + sum(1 for c in COPY if c >= 26)
NCHAN = 26 + sum(1 for c in COPY if c >= 26)


def shift_lanes(v, by):
    return pltpu.roll(v, by % 128, axis=1)


def velocity_of(chan):
    return LAT19[chan] if chan < 19 else LAT19[chan - 19]


def put(ref, chan, slot, xt, v):
    ref[chan, slot, pl.ds(8 + 8 * xt, 8), :] = v


def tile(ref, chan, s, xt):
    return ref[chan, s + 1, pl.ds(8 + 8 * xt, 8), :]


def moved_tile(ref, chan, s, xt):
    c = velocity_of(chan)
    return ref[COPY[chan], s + 1 - c[1], pl.ds(8 + 8 * xt - c[0], 8), :]


def put_all(ref, s, xt, post):
    for chan, v in enumerate(post):
        put(ref, chan, s + 1, xt, v)


def copies(ref):
    def roll_line(s, carry):
        for xt in range(XT):
            for chan in range(26):
                c = velocity_of(chan)
                if c[2]:
                    put(ref, COPY[chan], s + 1, xt, shift_lanes(tile(ref, chan, s, xt), c[2]))
        return carry

    for xt in range(XT):
        for chan in range(26):
            c = velocity_of(chan)
            if c[1] > 0:
                put(ref, COPY[chan], 0, xt, shift_lanes(tile(ref, chan, NS - 1, xt), c[2] + 32))
            if c[1] < 0:
                put(ref, COPY[chan], NS + 1, xt, shift_lanes(tile(ref, chan, 0, xt), c[2] - 32))
    lax.fori_loop(0, NS, roll_line, 0, unroll=True)


def moments(f):
    quad = []
    for k in (7, 11, 15):
        p, m = f[k] + f[k + 2], f[k + 1] + f[k + 3]
        quad.append((p + m, p - m, (f[k] - f[k + 2]) - (f[k + 1] - f[k + 3])))
    rho = f[0] + (f[1] + f[2]) + (f[3] + f[4]) + (f[5] + f[6])
    rho = rho + quad[0][0] + quad[1][0] + quad[2][0]
    mx = (f[1] - f[2]) + quad[0][1] + quad[1][1]
    my = (f[3] - f[4]) + quad[0][2] + quad[2][1]
    mz = (f[5] - f[6]) + quad[1][2] + quad[2][2]
    return rho, mx, my, mz


def inverse(v):
    r = pl.reciprocal(v, approx=True)
    return r * (2.0 - v * r)


def collide(f, g):
    rho, mx, my, mz = moments(f)
    inv = inverse(rho)
    mom = (mx, my, mz)
    u = [m * inv for m in mom]
    y = [(4.5 * W2) * m for m in mom]
    diag = [y[a] * u[a] for a in range(3)]
    o = [(3.0 * W2) * m for m in mom]
    base = W2 * rho - (diag[0] + diag[1] + diag[2]) * (1.0 / 3.0)
    t = [base + d for d in diag]
    post = [None] * 19
    post[0] = f[0] + 12.0 * base
    for a in range(3):
        e, od = t[a] + t[a], o[a] + o[a]
        post[1 + 2 * a] = f[1 + 2 * a] + (e + od)
        post[2 + 2 * a] = f[2 + 2 * a] + (e - od)
    for k, a, b in ((7, 0, 1), (11, 0, 2), (15, 1, 2)):
        e = t[a] + diag[b]
        cross = (y[a] + y[a]) * u[b]
        ep, em = e + cross, e - cross
        op, om = o[a] + o[b], o[a] - o[b]
        post[k] = f[k] + (ep + op)
        post[k + 1] = f[k + 1] + (ep - op)
        post[k + 2] = f[k + 2] + (em + om)
        post[k + 3] = f[k + 3] + (em - om)
    temp = g[0] + (g[1] + g[2]) + (g[3] + g[4]) + (g[5] + g[6])
    eq = (0.125 * OMG) * temp
    eq4 = (0.5 * OMG) * temp
    post.append(LAMG * g[0] + (eq + eq))
    for a in range(3):
        ua = eq4 * u[a]
        post.append(LAMG * g[1 + 2 * a] + (eq + ua))
        post.append(LAMG * g[2 + 2 * a] + (eq - ua))
    return post


def equilibrium(u):
    y = [(4.5 * KAPPA_0) * v for v in u]
    diag = [y[a] * u[a] for a in range(3)]
    o = [(3.0 * KAPPA_0) * v for v in u]
    base = KAPPA_0 - (diag[0] + diag[1] + diag[2]) * (1.0 / 3.0)
    t = [base + d for d in diag]
    f = [None] * 19
    f[0] = 12.0 * base
    for a in range(3):
        e, od = t[a] + t[a], o[a] + o[a]
        f[1 + 2 * a], f[2 + 2 * a] = e + od, e - od
    for k, a, b in ((7, 0, 1), (11, 0, 2), (15, 1, 2)):
        e = t[a] + diag[b]
        cross = (y[a] + y[a]) * u[b]
        ep, em = e + cross, e - cross
        op, om = o[a] + o[b], o[a] - o[b]
        f[k], f[k + 1], f[k + 2], f[k + 3] = ep + op, ep - op, em + om, em - om
    return f


def stream(src, wa, wb, s, xt):
    f = [tile(src, 0, s, xt)]
    g = [tile(src, 19, s, xt)]
    for i in range(1, 19):
        moved = moved_tile(src, i, s, xt)
        open_ = moved < BIG
        f.append(jnp.where(open_, moved, tile(src, OPP[i], s, xt)))
        if i < 7:
            back = tile(src, 19 + OPP[i], s, xt)
            c = LAT19[i]
            near = (c[2] % 3, s + 1 - c[1], pl.ds(8 + 8 * xt - c[0], 8))
            back = wa[near] * back + wb[near]
            g.append(jnp.where(open_, moved_tile(src, 19 + i, s, xt), back))
    return f, g


def window(zbase, side_one, own, side_two, end_one, end_two, temp_out, flow_out, part_out,
           stage, inp, pops, wa, wb, res):
    height = zbase[1]
    even_y, even_z = zbase[2] > 0.5, zbase[3] > 0.5

    def low_high(even, one, two):
        return jnp.where(even, two, one), jnp.where(even, one, two)

    for a in range(5):
        left, right = low_high(even_y, side_one[a], side_two[a])
        top, bot = low_high(even_z, end_one[a], end_two[a])
        blocks = (left, own[a, :, 0:192], own[a, :, 192:384], right)
        for q in range(4):
            r0 = 32 * q
            stage[a, r0 : r0 + 8, 0:192] = top[:, 192 * q : 192 * q + 192]
            stage[a, r0 + 8 : r0 + 24, 0:192] = blocks[q]
            stage[a, r0 + 24 : r0 + 32, 0:192] = bot[:, 192 * q : 192 * q + 192]
        inp[a, 0:16] = stage[a, :, 0:128].T.reshape(16, 8, 128)
        inp[a, 16:24] = stage[a, :, 128:256].T[0:64].reshape(8, 8, 128)

    lane = lax.broadcasted_iota(jnp.int32, (8, 128), 1)
    zin = lane % 32
    mine = (zin >= HALO) & (zin < 32 - HALO) & (lane >= 32) & (lane < 96)
    zpos = zbase[0] + zin.astype(jnp.float32)
    ramp = 0.5 - 0.75 * (zpos + 0.5) / height

    def first(s):
        for xt in range(XT):
            kind = inp[0, s * XT + xt]
            hot, cold = kind == 2.0, kind == 3.0
            sign = jnp.where(hot | cold, -1.0, 1.0)
            gain = jnp.where(hot, 0.125, jnp.where(cold, -0.125, 0.0))
            for ref, v in ((wa, sign), (wb, gain)):
                for chan in range(3):
                    put(ref, chan, s + 1, xt, shift_lanes(v, (0, 1, -1)[chan]) if chan else v)
                if s == 0:
                    put(ref, 0, NS + 1, xt, shift_lanes(v, -32))
                if s == NS - 1:
                    put(ref, 0, 0, xt, shift_lanes(v, 32))
            fluid = kind == 0.0
            u = [inp[2 + a, s * XT + xt] for a in range(3)]
            temp = ramp + 0.05 * inp[1, s * XT + xt]
            f = equilibrium(u)
            f = [jnp.where(fluid, v, jnp.nan) for v in f]
            eq, eq4 = 0.125 * temp, 0.5 * temp
            f.append(eq + eq)
            for a in range(3):
                ua = eq4 * u[a]
                f.append(eq + ua)
                f.append(eq - ua)
            put_all(pops.at[0], s, xt, f)

    for s in range(NS):
        first(s)
    copies(pops.at[0])

    def step(k, carry):
        src, dst = pops.at[lax.rem(k + 1, 2)], pops.at[lax.rem(k, 2)]

        def line(s, c):
            for xt in range(XT):
                f, g = stream(src, wa, wb, s, xt)
                put_all(dst, s, xt, collide(f, g))
            return c

        lax.fori_loop(0, NS, line, 0, unroll=4)
        copies(dst)
        return carry

    lax.fori_loop(1, STEPS, step, 0)
    src = pops.at[(STEPS - 1) % 2]

    def last(s, total):
        for xt in range(XT):
            f, g = stream(src, wa, wb, s, xt)
            rho, mx, my, mz = moments(f)
            fluid = f[0] < BIG
            inv = inverse(rho)
            kind = inp[0, s * XT + xt]
            walls = jnp.where(kind == 2.0, 0.5, jnp.where(kind == 3.0, -0.5, 0.0))
            temp = g[0] + (g[1] + g[2]) + (g[3] + g[4]) + (g[5] + g[6])
            temp = jnp.where(fluid, temp, walls)
            res[0, s * XT + xt] = temp
            for a, m in enumerate((mx, my, mz)):
                res[1 + a, s * XT + xt] = jnp.where(fluid, m * inv, 0.0)
            heated = fluid & mine & (wb[0, s, pl.ds(8 + 8 * xt, 8), :] == 0.125)
            total = total + jnp.where(heated, 0.5 - temp, 0.0)
        return total

    total = lax.fori_loop(0, NS, last, jnp.zeros((8, 128), jnp.float32), unroll=True)
    part_out[...] = jnp.full(part_out.shape, jnp.sum(total), jnp.float32)
    for o in range(4):
        one = res[o, 0:16].reshape(128, 128).T
        two = res[o, 16:32].reshape(128, 128).T
        for q in (1, 2):
            rows = slice(32 * q + 8, 32 * q + 24)
            at = 192 * (q - 1)
            val = jnp.concatenate([one[rows], two[rows, 0:64]], axis=1)
            if o == 0:
                temp_out[:, at : at + 192] = val
            else:
                flow_out[o - 1, :, at : at + 192] = val


SCRATCH = [
    pltpu.VMEM((5, 128, 256), jnp.float32),
    pltpu.VMEM((5, NS * XT, 8, 128), jnp.float32),
    pltpu.VMEM((2, NCHAN, NS + 2, ROWS, 128), jnp.float32),
    pltpu.VMEM((3, NS + 2, ROWS, 128), jnp.float32),
    pltpu.VMEM((3, NS + 2, ROWS, 128), jnp.float32),
    pltpu.VMEM((4, 32, 8, 128), jnp.float32),
]


def all_sum(part, axes, count, first):
    order = [[(i + first) % count for i in range(count)]]
    parts = lax.all_to_all(part, axes, 0, 0, tiled=True, axis_index_groups=order)
    return jnp.sum(parts, axis=0)


def swap(axis, count, even, head, tail):
    near = [(i, i ^ 1) for i in range(count)]
    far = [(i, (((i + 1) % count) ^ 1) - 1) for i in range(count)]
    far = [(i, j % count) for i, j in far]
    two = lax.ppermute(jnp.where(even, head, tail), axis, far)
    one = lax.ppermute(jnp.where(even, tail, head), axis, near)
    return one, two


def make_body(gz, gy, near, far, n_near, n_far, n_gz, n_gy):
    def body(cell_type, perturb, velocity):
        slab, cells = cell_type.shape
        height = slab * n_gz
        own = jnp.concatenate(
            [
                cell_type.astype(jnp.float32)[None],
                perturb.astype(jnp.float32)[None],
                velocity,
            ]
        )
        rim = HALO * NX
        even_y = (lax.axis_index(gy) & 1) == 0
        even_z = (lax.axis_index(gz[-1]) & 1) == 0
        sides = swap(gy, n_gy, even_y, own[:, :, :rim], own[:, :, cells - rim :])
        left = jnp.where(even_y, sides[1], sides[0])
        right = jnp.where(even_y, sides[0], sides[1])
        wide = jnp.concatenate([left, own, right], axis=2)
        ends = swap(gz, n_gz, even_z, wide[:, :HALO], wide[:, slab - HALO :])
        zbase = jnp.stack(
            [
                (lax.axis_index(gz) * slab - HALO).astype(jnp.float32),
                jnp.float32(height),
                even_y.astype(jnp.float32),
                even_z.astype(jnp.float32),
            ]
        )
        vmem = pl.BlockSpec(memory_space=pltpu.VMEM)
        f32 = jnp.float32
        temp, flow, part = pl.pallas_call(
            window,
            in_specs=[pl.BlockSpec(memory_space=pltpu.SMEM)] + [vmem] * 5,
            out_specs=[vmem] * 3,
            out_shape=[
                jax.ShapeDtypeStruct((slab, cells), f32),
                jax.ShapeDtypeStruct((3, slab, cells), f32),
                jax.ShapeDtypeStruct((n_near, 128), f32),
            ],
            scratch_shapes=SCRATCH,
            compiler_params=pltpu.CompilerParams(vmem_limit_bytes=40 * 1024 * 1024),
            name="lattice_window",
        )(zbase, sides[0], own, sides[1], ends[0], ends[1])
        line = all_sum(part, near, n_near, n_gy + 5 * n_gy // 8)
        line = all_sum(jnp.broadcast_to(line, (n_far, 128)), far, n_far, 9 * n_far // 16)
        return temp, flow, line[0] * (2.0 / (NX * height))

    return body


def solution(mesh):
    n_gz, n_gy = mesh.shape["gz"], mesh.shape["gy"]
    z = n_gz // 4
    fine = Mesh(
        np.asarray(mesh.devices).reshape(2, z, 2, n_gy),
        ("yl", "z", "core", "gy"),
    )
    gz = ("yl", "z", "core")
    near = ("yl", "core", "gy")
    body = make_body(gz, "gy", near, "z", 4 * n_gy, z, n_gz, n_gy)
    return jax.shard_map(
        body,
        mesh=fine,
        in_specs=(P(gz, "gy"), P(gz, "gy"), P(None, gz, "gy")),
        out_specs=(P(gz, "gy"), P(None, gz, "gy"), P()),
        check_vma=False,
    )
```

```python
import numpy as np

import jax
import jax.numpy as jnp
from jax import lax
from jax.experimental import pallas as pl
from jax.experimental.pallas import tpu as pltpu
from jax.sharding import Mesh, PartitionSpec as P

NX = 24
STEPS = 8
HALO = STEPS
TAU_F = 0.52
TAU_G = 0.5376
LAT19 = [
    (0, 0, 0),
    (1, 0, 0),
    (-1, 0, 0),
    (0, 1, 0),
    (0, -1, 0),
    (0, 0, 1),
    (0, 0, -1),
    (1, 1, 0),
    (-1, -1, 0),
    (1, -1, 0),
    (-1, 1, 0),
    (1, 0, 1),
    (-1, 0, -1),
    (1, 0, -1),
    (-1, 0, 1),
    (0, 1, 1),
    (0, -1, -1),
    (0, 1, -1),
    (0, -1, 1),
]
WGT19 = [1.0 / 3.0] + [1.0 / 18.0] * 6 + [1.0 / 36.0] * 12
LAT7 = LAT19[:7]
WGT7 = [0.25] + [0.125] * 6
OPP = [LAT19.index(tuple(-v for v in c)) for c in LAT19]

KAPPA = -1.0 / (1.0 - TAU_F)
W2 = KAPPA / 36.0
KAPPA_0 = 1.0 / 36.0 / (1.0 - 1.0 / TAU_F)
OMG = 1.0 / TAU_G
LAMG = 1.0 - OMG
BIG = 1e30

NS = 8
XT = NX // 8
ROWS = 40


COPY = list(range(26))
for _i in range(1, 19):
    if LAT19[_i][2]:
        COPY[_i] = 26 + sum(1 for c in COPY if c >= 26)
for _i in range(1, 7):
    if LAT19[_i][2]:
        COPY[19 + _i] = 26 + sum(1 for c in COPY if c >= 26)
NCHAN = 26 + sum(1 for c in COPY if c >= 26)


def shift_lanes(v, by):
    return pltpu.roll(v, by % 128, axis=1)


def velocity_of(chan):
    return LAT19[chan] if chan < 19 else LAT19[chan - 19]


def put(ref, chan, slot, xt, v):
    ref[chan, slot, pl.ds(8 + 8 * xt, 8), :] = v


def tile(ref, chan, s, xt):
    return ref[chan, s + 1, pl.ds(8 + 8 * xt, 8), :]


def moved_tile(ref, chan, s, xt):
    c = velocity_of(chan)
    return ref[COPY[chan], s + 1 - c[1], pl.ds(8 + 8 * xt - c[0], 8), :]


def put_all(ref, s, xt, post):
    for chan, v in enumerate(post):
        put(ref, chan, s + 1, xt, v)


def copies(ref):
    def roll_line(s, carry):
        for xt in range(XT):
            for chan in range(26):
                c = velocity_of(chan)
                if c[2]:
                    put(ref, COPY[chan], s + 1, xt, shift_lanes(tile(ref, chan, s, xt), c[2]))
        return carry

    for xt in range(XT):
        for chan in range(26):
            c = velocity_of(chan)
            if c[1] > 0:
                put(ref, COPY[chan], 0, xt, shift_lanes(tile(ref, chan, NS - 1, xt), c[2] + 32))
            if c[1] < 0:
                put(ref, COPY[chan], NS + 1, xt, shift_lanes(tile(ref, chan, 0, xt), c[2] - 32))
    lax.fori_loop(0, NS, roll_line, 0, unroll=True)


def moments(f):
    quad = []
    for k in (7, 11, 15):
        p, m = f[k] + f[k + 2], f[k + 1] + f[k + 3]
        quad.append((p + m, p - m, (f[k] - f[k + 2]) - (f[k + 1] - f[k + 3])))
    rho = f[0] + (f[1] + f[2]) + (f[3] + f[4]) + (f[5] + f[6])
    rho = rho + quad[0][0] + quad[1][0] + quad[2][0]
    mx = (f[1] - f[2]) + quad[0][1] + quad[1][1]
    my = (f[3] - f[4]) + quad[0][2] + quad[2][1]
    mz = (f[5] - f[6]) + quad[1][2] + quad[2][2]
    return rho, mx, my, mz


def inverse(v):
    r = pl.reciprocal(v, approx=True)
    return r * (2.0 - v * r)


def collide(f, g):
    rho, mx, my, mz = moments(f)
    inv = inverse(rho)
    mom = (mx, my, mz)
    u = [m * inv for m in mom]
    y = [(4.5 * W2) * m for m in mom]
    diag = [y[a] * u[a] for a in range(3)]
    o = [(3.0 * W2) * m for m in mom]
    base = W2 * rho - (diag[0] + diag[1] + diag[2]) * (1.0 / 3.0)
    t = [base + d for d in diag]
    post = [None] * 19
    post[0] = f[0] + 12.0 * base
    for a in range(3):
        e, od = t[a] + t[a], o[a] + o[a]
        post[1 + 2 * a] = f[1 + 2 * a] + (e + od)
        post[2 + 2 * a] = f[2 + 2 * a] + (e - od)
    for k, a, b in ((7, 0, 1), (11, 0, 2), (15, 1, 2)):
        e = t[a] + diag[b]
        cross = (y[a] + y[a]) * u[b]
        ep, em = e + cross, e - cross
        op, om = o[a] + o[b], o[a] - o[b]
        post[k] = f[k] + (ep + op)
        post[k + 1] = f[k + 1] + (ep - op)
        post[k + 2] = f[k + 2] + (em + om)
        post[k + 3] = f[k + 3] + (em - om)
    temp = g[0] + (g[1] + g[2]) + (g[3] + g[4]) + (g[5] + g[6])
    eq = (0.125 * OMG) * temp
    eq4 = (0.5 * OMG) * temp
    post.append(LAMG * g[0] + (eq + eq))
    for a in range(3):
        ua = eq4 * u[a]
        post.append(LAMG * g[1 + 2 * a] + (eq + ua))
        post.append(LAMG * g[2 + 2 * a] + (eq - ua))
    return post


def equilibrium(u):
    y = [(4.5 * KAPPA_0) * v for v in u]
    diag = [y[a] * u[a] for a in range(3)]
    o = [(3.0 * KAPPA_0) * v for v in u]
    base = KAPPA_0 - (diag[0] + diag[1] + diag[2]) * (1.0 / 3.0)
    t = [base + d for d in diag]
    f = [None] * 19
    f[0] = 12.0 * base
    for a in range(3):
        e, od = t[a] + t[a], o[a] + o[a]
        f[1 + 2 * a], f[2 + 2 * a] = e + od, e - od
    for k, a, b in ((7, 0, 1), (11, 0, 2), (15, 1, 2)):
        e = t[a] + diag[b]
        cross = (y[a] + y[a]) * u[b]
        ep, em = e + cross, e - cross
        op, om = o[a] + o[b], o[a] - o[b]
        f[k], f[k + 1], f[k + 2], f[k + 3] = ep + op, ep - op, em + om, em - om
    return f


def stream(src, wa, wb, s, xt):
    f = [tile(src, 0, s, xt)]
    g = [tile(src, 19, s, xt)]
    for i in range(1, 19):
        moved = moved_tile(src, i, s, xt)
        open_ = moved < BIG
        f.append(jnp.where(open_, moved, tile(src, OPP[i], s, xt)))
        if i < 7:
            back = tile(src, 19 + OPP[i], s, xt)
            c = LAT19[i]
            near = (c[2] % 3, s + 1 - c[1], pl.ds(8 + 8 * xt - c[0], 8))
            back = wa[near] * back + wb[near]
            g.append(jnp.where(open_, moved_tile(src, 19 + i, s, xt), back))
    return f, g


def window(zbase, side_one, own, side_two, end_one, end_two, temp_out, flow_out, part_out,
           stage, inp, pops, wa, wb, res):
    height = zbase[1]
    even_y, even_z = zbase[2] > 0.5, zbase[3] > 0.5

    def low_high(even, one, two):
        return jnp.where(even, two, one), jnp.where(even, one, two)

    for a in range(5):
        left, right = low_high(even_y, side_one[a], side_two[a])
        top, bot = low_high(even_z, end_one[a], end_two[a])
        blocks = (left, own[a, :, 0:192], own[a, :, 192:384], right)
        for q in range(4):
            r0 = 32 * q
            stage[a, r0 : r0 + 8, 0:192] = top[:, 192 * q : 192 * q + 192]
            stage[a, r0 + 8 : r0 + 24, 0:192] = blocks[q]
            stage[a, r0 + 24 : r0 + 32, 0:192] = bot[:, 192 * q : 192 * q + 192]
        inp[a, 0:16] = stage[a, :, 0:128].T.reshape(16, 8, 128)
        inp[a, 16:24] = stage[a, :, 128:256].T[0:64].reshape(8, 8, 128)

    lane = lax.broadcasted_iota(jnp.int32, (8, 128), 1)
    zin = lane % 32
    mine = (zin >= HALO) & (zin < 32 - HALO) & (lane >= 32) & (lane < 96)
    zpos = zbase[0] + zin.astype(jnp.float32)
    ramp = 0.5 - 0.75 * (zpos + 0.5) / height

    def first(s):
        for xt in range(XT):
            kind = inp[0, s * XT + xt]
            hot, cold = kind == 2.0, kind == 3.0
            sign = jnp.where(hot | cold, -1.0, 1.0)
            gain = jnp.where(hot, 0.125, jnp.where(cold, -0.125, 0.0))
            for ref, v in ((wa, sign), (wb, gain)):
                for chan in range(3):
                    put(ref, chan, s + 1, xt, shift_lanes(v, (0, 1, -1)[chan]) if chan else v)
                if s == 0:
                    put(ref, 0, NS + 1, xt, shift_lanes(v, -32))
                if s == NS - 1:
                    put(ref, 0, 0, xt, shift_lanes(v, 32))
            fluid = kind == 0.0
            u = [inp[2 + a, s * XT + xt] for a in range(3)]
            temp = ramp + 0.05 * inp[1, s * XT + xt]
            f = equilibrium(u)
            f = [jnp.where(fluid, v, jnp.nan) for v in f]
            eq, eq4 = 0.125 * temp, 0.5 * temp
            f.append(eq + eq)
            for a in range(3):
                ua = eq4 * u[a]
                f.append(eq + ua)
                f.append(eq - ua)
            put_all(pops.at[0], s, xt, f)

    for s in range(NS):
        first(s)
    copies(pops.at[0])

    def step(k, carry):
        src, dst = pops.at[lax.rem(k + 1, 2)], pops.at[lax.rem(k, 2)]

        def line(s, c):
            for xt in range(XT):
                f, g = stream(src, wa, wb, s, xt)
                put_all(dst, s, xt, collide(f, g))
            return c

        lax.fori_loop(0, NS, line, 0, unroll=4)
        copies(dst)
        return carry

    lax.fori_loop(1, STEPS, step, 0)
    src = pops.at[(STEPS - 1) % 2]

    def last(s, total):
        for xt in range(XT):
            f, g = stream(src, wa, wb, s, xt)
            rho, mx, my, mz = moments(f)
            fluid = f[0] < BIG
            inv = inverse(rho)
            kind = inp[0, s * XT + xt]
            walls = jnp.where(kind == 2.0, 0.5, jnp.where(kind == 3.0, -0.5, 0.0))
            temp = g[0] + (g[1] + g[2]) + (g[3] + g[4]) + (g[5] + g[6])
            temp = jnp.where(fluid, temp, walls)
            res[0, s * XT + xt] = temp
            for a, m in enumerate((mx, my, mz)):
                res[1 + a, s * XT + xt] = jnp.where(fluid, m * inv, 0.0)
            heated = fluid & mine & (wb[0, s, pl.ds(8 + 8 * xt, 8), :] == 0.125)
            total = total + jnp.where(heated, 0.5 - temp, 0.0)
        return total

    total = lax.fori_loop(0, NS, last, jnp.zeros((8, 128), jnp.float32), unroll=True)
    part_out[...] = jnp.full(part_out.shape, jnp.sum(total), jnp.float32)
    for o in range(4):
        one = res[o, 0:16].reshape(128, 128).T
        two = res[o, 16:32].reshape(128, 128).T
        for q in (1, 2):
            rows = slice(32 * q + 8, 32 * q + 24)
            at = 192 * (q - 1)
            val = jnp.concatenate([one[rows], two[rows, 0:64]], axis=1)
            if o == 0:
                temp_out[:, at : at + 192] = val
            else:
                flow_out[o - 1, :, at : at + 192] = val


SCRATCH = [
    pltpu.VMEM((5, 128, 256), jnp.float32),
    pltpu.VMEM((5, NS * XT, 8, 128), jnp.float32),
    pltpu.VMEM((2, NCHAN, NS + 2, ROWS, 128), jnp.float32),
    pltpu.VMEM((3, NS + 2, ROWS, 128), jnp.float32),
    pltpu.VMEM((3, NS + 2, ROWS, 128), jnp.float32),
    pltpu.VMEM((4, 32, 8, 128), jnp.float32),
]


def all_sum(part, axes, count, first):
    order = [[(i + first) % count for i in range(count)]]
    parts = lax.all_to_all(part, axes, 0, 0, tiled=True, axis_index_groups=order)
    return jnp.sum(parts, axis=0)


def swap(axis, count, even, head, tail):
    near = [(i, i ^ 1) for i in range(count)]
    far = [(i, ((i + 1) ^ 1) - 1) for i in range(1, count - 1)]
    two = lax.ppermute(jnp.where(even, head, tail), axis, far)
    one = lax.ppermute(jnp.where(even, tail, head), axis, near)
    return one, two


def make_body(gz, gy, near, far, n_near, n_far, n_gz, n_gy):
    def body(cell_type, perturb, velocity):
        slab, cells = cell_type.shape
        height = slab * n_gz
        own = jnp.concatenate(
            [
                cell_type.astype(jnp.float32)[None],
                perturb.astype(jnp.float32)[None],
                velocity,
            ]
        )
        rim = HALO * NX
        even_y = (lax.axis_index(gy) & 1) == 0
        even_z = (lax.axis_index(gz[-1]) & 1) == 0
        sides = swap(gy, n_gy, even_y, own[:, :, :rim], own[:, :, cells - rim :])
        left = jnp.where(even_y, sides[1], sides[0])
        right = jnp.where(even_y, sides[0], sides[1])
        wide = jnp.concatenate([left, own, right], axis=2)
        ends = swap(gz, n_gz, even_z, wide[:, :HALO], wide[:, slab - HALO :])
        zbase = jnp.stack(
            [
                (lax.axis_index(gz) * slab - HALO).astype(jnp.float32),
                jnp.float32(height),
                even_y.astype(jnp.float32),
                even_z.astype(jnp.float32),
            ]
        )
        vmem = pl.BlockSpec(memory_space=pltpu.VMEM)
        f32 = jnp.float32
        temp, flow, part = pl.pallas_call(
            window,
            in_specs=[pl.BlockSpec(memory_space=pltpu.SMEM)] + [vmem] * 5,
            out_specs=[vmem] * 3,
            out_shape=[
                jax.ShapeDtypeStruct((slab, cells), f32),
                jax.ShapeDtypeStruct((3, slab, cells), f32),
                jax.ShapeDtypeStruct((n_near, 128), f32),
            ],
            scratch_shapes=SCRATCH,
            compiler_params=pltpu.CompilerParams(vmem_limit_bytes=40 * 1024 * 1024),
            name="lattice_window",
        )(zbase, sides[0], own, sides[1], ends[0], ends[1])
        line = all_sum(part, near, n_near, n_gy + 5 * n_gy // 8)
        line = all_sum(jnp.broadcast_to(line, (n_far, 128)), far, n_far, 9 * n_far // 16)
        return temp, flow, line[0] * (2.0 / (NX * height))

    return body


def solution(mesh):
    n_gz, n_gy = mesh.shape["gz"], mesh.shape["gy"]
    z = n_gz // 4
    fine = Mesh(
        np.asarray(mesh.devices).reshape(2, z, 2, n_gy),
        ("yl", "z", "core", "gy"),
    )
    gz = ("yl", "z", "core")
    near = ("yl", "core", "gy")
    body = make_body(gz, "gy", near, "z", 4 * n_gy, z, n_gz, n_gy)
    return jax.shard_map(
        body,
        mesh=fine,
        in_specs=(P(gz, "gy"), P(gz, "gy"), P(None, gz, "gy")),
        out_specs=(P(gz, "gy"), P(None, gz, "gy"), P()),
        check_vma=False,
    )
```

```python
import numpy as np

import jax
import jax.numpy as jnp
from jax import lax
from jax.experimental import pallas as pl
from jax.experimental.pallas import tpu as pltpu
from jax.sharding import Mesh, PartitionSpec as P

NX = 24
STEPS = 8
HALO = STEPS
TAU_F = 0.52
TAU_G = 0.5376
LAT19 = [
    (0, 0, 0),
    (1, 0, 0),
    (-1, 0, 0),
    (0, 1, 0),
    (0, -1, 0),
    (0, 0, 1),
    (0, 0, -1),
    (1, 1, 0),
    (-1, -1, 0),
    (1, -1, 0),
    (-1, 1, 0),
    (1, 0, 1),
    (-1, 0, -1),
    (1, 0, -1),
    (-1, 0, 1),
    (0, 1, 1),
    (0, -1, -1),
    (0, 1, -1),
    (0, -1, 1),
]
WGT19 = [1.0 / 3.0] + [1.0 / 18.0] * 6 + [1.0 / 36.0] * 12
LAT7 = LAT19[:7]
WGT7 = [0.25] + [0.125] * 6
OPP = [LAT19.index(tuple(-v for v in c)) for c in LAT19]

KAPPA = -1.0 / (1.0 - TAU_F)
W2 = KAPPA / 36.0
KAPPA_0 = 1.0 / 36.0 / (1.0 - 1.0 / TAU_F)
OMG = 1.0 / TAU_G
LAMG = 1.0 - OMG
BIG = 1e30

NS = 8
XT = NX // 8
ROWS = 40


COPY = list(range(26))
for _i in range(1, 19):
    if LAT19[_i][2]:
        COPY[_i] = 26 + sum(1 for c in COPY if c >= 26)
for _i in range(1, 7):
    if LAT19[_i][2]:
        COPY[19 + _i] = 26 + sum(1 for c in COPY if c >= 26)
NCHAN = 26 + sum(1 for c in COPY if c >= 26)


def shift_lanes(v, by):
    return pltpu.roll(v, by % 128, axis=1)


def velocity_of(chan):
    return LAT19[chan] if chan < 19 else LAT19[chan - 19]


def put(ref, chan, slot, xt, v):
    ref[chan, slot, pl.ds(8 + 8 * xt, 8), :] = v


def tile(ref, chan, s, xt):
    return ref[chan, s + 1, pl.ds(8 + 8 * xt, 8), :]


def moved_tile(ref, chan, s, xt):
    c = velocity_of(chan)
    return ref[COPY[chan], s + 1 - c[1], pl.ds(8 + 8 * xt - c[0], 8), :]


def put_all(ref, s, xt, post):
    for chan, v in enumerate(post):
        put(ref, chan, s + 1, xt, v)


def copies(ref):
    def roll_line(s, carry):
        for xt in range(XT):
            for chan in range(26):
                c = velocity_of(chan)
                if c[2]:
                    put(ref, COPY[chan], s + 1, xt, shift_lanes(tile(ref, chan, s, xt), c[2]))
        return carry

    for xt in range(XT):
        for chan in range(26):
            c = velocity_of(chan)
            if c[1] > 0:
                put(ref, COPY[chan], 0, xt, shift_lanes(tile(ref, chan, NS - 1, xt), c[2] + 32))
            if c[1] < 0:
                put(ref, COPY[chan], NS + 1, xt, shift_lanes(tile(ref, chan, 0, xt), c[2] - 32))
    lax.fori_loop(0, NS, roll_line, 0, unroll=True)


def moments(f):
    quad = []
    for k in (7, 11, 15):
        p, m = f[k] + f[k + 2], f[k + 1] + f[k + 3]
        quad.append((p + m, p - m, (f[k] - f[k + 2]) - (f[k + 1] - f[k + 3])))
    rho = f[0] + (f[1] + f[2]) + (f[3] + f[4]) + (f[5] + f[6])
    rho = rho + quad[0][0] + quad[1][0] + quad[2][0]
    mx = (f[1] - f[2]) + quad[0][1] + quad[1][1]
    my = (f[3] - f[4]) + quad[0][2] + quad[2][1]
    mz = (f[5] - f[6]) + quad[1][2] + quad[2][2]
    return rho, mx, my, mz


def inverse(v):
    r = pl.reciprocal(v, approx=True)
    return r * (2.0 - v * r)


def collide(f, g):
    rho, mx, my, mz = moments(f)
    inv = inverse(rho)
    mom = (mx, my, mz)
    u = [m * inv for m in mom]
    y = [(4.5 * W2) * m for m in mom]
    diag = [y[a] * u[a] for a in range(3)]
    o = [(3.0 * W2) * m for m in mom]
    base = W2 * rho - (diag[0] + diag[1] + diag[2]) * (1.0 / 3.0)
    t = [base + d for d in diag]
    post = [None] * 19
    post[0] = f[0] + 12.0 * base
    for a in range(3):
        e, od = t[a] + t[a], o[a] + o[a]
        post[1 + 2 * a] = f[1 + 2 * a] + (e + od)
        post[2 + 2 * a] = f[2 + 2 * a] + (e - od)
    for k, a, b in ((7, 0, 1), (11, 0, 2), (15, 1, 2)):
        e = t[a] + diag[b]
        cross = (y[a] + y[a]) * u[b]
        ep, em = e + cross, e - cross
        op, om = o[a] + o[b], o[a] - o[b]
        post[k] = f[k] + (ep + op)
        post[k + 1] = f[k + 1] + (ep - op)
        post[k + 2] = f[k + 2] + (em + om)
        post[k + 3] = f[k + 3] + (em - om)
    temp = g[0] + (g[1] + g[2]) + (g[3] + g[4]) + (g[5] + g[6])
    eq = (0.125 * OMG) * temp
    eq4 = (0.5 * OMG) * temp
    post.append(LAMG * g[0] + (eq + eq))
    for a in range(3):
        ua = eq4 * u[a]
        post.append(LAMG * g[1 + 2 * a] + (eq + ua))
        post.append(LAMG * g[2 + 2 * a] + (eq - ua))
    return post


def equilibrium(u):
    y = [(4.5 * KAPPA_0) * v for v in u]
    diag = [y[a] * u[a] for a in range(3)]
    o = [(3.0 * KAPPA_0) * v for v in u]
    base = KAPPA_0 - (diag[0] + diag[1] + diag[2]) * (1.0 / 3.0)
    t = [base + d for d in diag]
    f = [None] * 19
    f[0] = 12.0 * base
    for a in range(3):
        e, od = t[a] + t[a], o[a] + o[a]
        f[1 + 2 * a], f[2 + 2 * a] = e + od, e - od
    for k, a, b in ((7, 0, 1), (11, 0, 2), (15, 1, 2)):
        e = t[a] + diag[b]
        cross = (y[a] + y[a]) * u[b]
        ep, em = e + cross, e - cross
        op, om = o[a] + o[b], o[a] - o[b]
        f[k], f[k + 1], f[k + 2], f[k + 3] = ep + op, ep - op, em + om, em - om
    return f


def stream(src, wa, wb, s, xt):
    f = [tile(src, 0, s, xt)]
    g = [tile(src, 19, s, xt)]
    for i in range(1, 19):
        moved = moved_tile(src, i, s, xt)
        open_ = moved < BIG
        f.append(jnp.where(open_, moved, tile(src, OPP[i], s, xt)))
        if i < 7:
            back = tile(src, 19 + OPP[i], s, xt)
            c = LAT19[i]
            near = (c[2] % 3, s + 1 - c[1], pl.ds(8 + 8 * xt - c[0], 8))
            back = wa[near] * back + wb[near]
            g.append(jnp.where(open_, moved_tile(src, 19 + i, s, xt), back))
    return f, g


def window(zbase, side_one, tall, side_two, temp_out, flow_out, part_out,
           stage, inp, pops, wa, wb, res):
    height = zbase[1]
    even_y = zbase[2] > 0.5
    for a in range(5):
        left = jnp.where(even_y, side_two[a], side_one[a])
        right = jnp.where(even_y, side_one[a], side_two[a])
        blocks = (left, tall[a, :, 0:192], tall[a, :, 192:384], right)
        for q in range(4):
            stage[a, 32 * q : 32 * q + 32, 0:192] = blocks[q]
        inp[a, 0:16] = stage[a, :, 0:128].T.reshape(16, 8, 128)
        inp[a, 16:24] = stage[a, :, 128:256].T[0:64].reshape(8, 8, 128)

    lane = lax.broadcasted_iota(jnp.int32, (8, 128), 1)
    zin = lane % 32
    mine = (zin >= HALO) & (zin < 32 - HALO) & (lane >= 32) & (lane < 96)
    zpos = zbase[0] + zin.astype(jnp.float32)
    ramp = 0.5 - 0.75 * (zpos + 0.5) / height

    def first(s):
        for xt in range(XT):
            kind = inp[0, s * XT + xt]
            hot, cold = kind == 2.0, kind == 3.0
            sign = jnp.where(hot | cold, -1.0, 1.0)
            gain = jnp.where(hot, 0.125, jnp.where(cold, -0.125, 0.0))
            for ref, v in ((wa, sign), (wb, gain)):
                for chan in range(3):
                    put(ref, chan, s + 1, xt, shift_lanes(v, (0, 1, -1)[chan]) if chan else v)
                if s == 0:
                    put(ref, 0, NS + 1, xt, shift_lanes(v, -32))
                if s == NS - 1:
                    put(ref, 0, 0, xt, shift_lanes(v, 32))
            fluid = kind == 0.0
            u = [inp[2 + a, s * XT + xt] for a in range(3)]
            temp = ramp + 0.05 * inp[1, s * XT + xt]
            f = equilibrium(u)
            f = [jnp.where(fluid, v, jnp.nan) for v in f]
            eq, eq4 = 0.125 * temp, 0.5 * temp
            f.append(eq + eq)
            for a in range(3):
                ua = eq4 * u[a]
                f.append(eq + ua)
                f.append(eq - ua)
            put_all(pops.at[0], s, xt, f)

    for s in range(NS):
        first(s)
    copies(pops.at[0])

    def step(k, carry):
        src, dst = pops.at[lax.rem(k + 1, 2)], pops.at[lax.rem(k, 2)]

        def line(s, c):
            for xt in range(XT):
                f, g = stream(src, wa, wb, s, xt)
                put_all(dst, s, xt, collide(f, g))
            return c

        lax.fori_loop(0, NS, line, 0, unroll=4)
        copies(dst)
        return carry

    lax.fori_loop(1, STEPS, step, 0)
    src = pops.at[(STEPS - 1) % 2]

    def last(s, total):
        for xt in range(XT):
            f, g = stream(src, wa, wb, s, xt)
            rho, mx, my, mz = moments(f)
            fluid = f[0] < BIG
            inv = inverse(rho)
            kind = inp[0, s * XT + xt]
            walls = jnp.where(kind == 2.0, 0.5, jnp.where(kind == 3.0, -0.5, 0.0))
            temp = g[0] + (g[1] + g[2]) + (g[3] + g[4]) + (g[5] + g[6])
            temp = jnp.where(fluid, temp, walls)
            res[0, s * XT + xt] = temp
            for a, m in enumerate((mx, my, mz)):
                res[1 + a, s * XT + xt] = jnp.where(fluid, m * inv, 0.0)
            heated = fluid & mine & (wb[0, s, pl.ds(8 + 8 * xt, 8), :] == 0.125)
            total = total + jnp.where(heated, 0.5 - temp, 0.0)
        return total

    total = lax.fori_loop(0, NS, last, jnp.zeros((8, 128), jnp.float32), unroll=True)
    part_out[...] = jnp.full(part_out.shape, jnp.sum(total), jnp.float32)
    for o in range(4):
        one = res[o, 0:16].reshape(128, 128).T
        two = res[o, 16:32].reshape(128, 128).T
        for q in (1, 2):
            rows = slice(32 * q + 8, 32 * q + 24)
            at = 192 * (q - 1)
            val = jnp.concatenate([one[rows], two[rows, 0:64]], axis=1)
            if o == 0:
                temp_out[:, at : at + 192] = val
            else:
                flow_out[o - 1, :, at : at + 192] = val


SCRATCH = [
    pltpu.VMEM((5, 128, 256), jnp.float32),
    pltpu.VMEM((5, NS * XT, 8, 128), jnp.float32),
    pltpu.VMEM((2, NCHAN, NS + 2, ROWS, 128), jnp.float32),
    pltpu.VMEM((3, NS + 2, ROWS, 128), jnp.float32),
    pltpu.VMEM((3, NS + 2, ROWS, 128), jnp.float32),
    pltpu.VMEM((4, 32, 8, 128), jnp.float32),
]


def all_sum(part, axes, count, first):
    order = [[(i + first) % count for i in range(count)]]
    parts = lax.all_to_all(part, axes, 0, 0, tiled=True, axis_index_groups=order)
    return jnp.sum(parts, axis=0)


def swap(axis, count, even, head, tail):
    near = [(i, i ^ 1) for i in range(count)]
    far = [(i, ((i + 1) ^ 1) - 1) for i in range(1, count - 1)]
    two = lax.ppermute(jnp.where(even, head, tail), axis, far)
    one = lax.ppermute(jnp.where(even, tail, head), axis, near)
    return one, two


def make_body(gz, gy, near, far, n_near, n_far, n_gz, n_gy):
    def body(cell_type, perturb, velocity):
        slab, cells = cell_type.shape
        height = slab * n_gz
        own = jnp.concatenate(
            [
                cell_type.astype(jnp.float32)[None],
                perturb.astype(jnp.float32)[None],
                velocity,
            ]
        )
        rim = HALO * NX
        even_y = (lax.axis_index(gy) & 1) == 0
        even_z = (lax.axis_index(gz[-1]) & 1) == 0
        ends = swap(gz, n_gz, even_z, own[:, :HALO], own[:, slab - HALO :])
        top = jnp.where(even_z, ends[1], ends[0])
        bot = jnp.where(even_z, ends[0], ends[1])
        tall = jnp.concatenate([top, own, bot], axis=1)
        sides = swap(gy, n_gy, even_y, tall[:, :, :rim], tall[:, :, cells - rim :])
        zbase = jnp.stack(
            [
                (lax.axis_index(gz) * slab - HALO).astype(jnp.float32),
                jnp.float32(height),
                even_y.astype(jnp.float32),
            ]
        )
        vmem = pl.BlockSpec(memory_space=pltpu.VMEM)
        f32 = jnp.float32
        temp, flow, part = pl.pallas_call(
            window,
            in_specs=[pl.BlockSpec(memory_space=pltpu.SMEM)] + [vmem] * 3,
            out_specs=[vmem] * 3,
            out_shape=[
                jax.ShapeDtypeStruct((slab, cells), f32),
                jax.ShapeDtypeStruct((3, slab, cells), f32),
                jax.ShapeDtypeStruct((n_near, 128), f32),
            ],
            scratch_shapes=SCRATCH,
            compiler_params=pltpu.CompilerParams(vmem_limit_bytes=40 * 1024 * 1024),
            name="lattice_window",
        )(zbase, sides[0], tall, sides[1])
        line = all_sum(part, near, n_near, n_gy + 5 * n_gy // 8)
        line = all_sum(jnp.broadcast_to(line, (n_far, 128)), far, n_far, 9 * n_far // 16)
        return temp, flow, line[0] * (2.0 / (NX * height))

    return body


def solution(mesh):
    n_gz, n_gy = mesh.shape["gz"], mesh.shape["gy"]
    z = n_gz // 4
    fine = Mesh(
        np.asarray(mesh.devices).reshape(2, z, 2, n_gy),
        ("yl", "z", "core", "gy"),
    )
    gz = ("yl", "z", "core")
    near = ("yl", "core", "gy")
    body = make_body(gz, "gy", near, "z", 4 * n_gy, z, n_gz, n_gy)
    return jax.shard_map(
        body,
        mesh=fine,
        in_specs=(P(gz, "gy"), P(gz, "gy"), P(None, gz, "gy")),
        out_specs=(P(gz, "gy"), P(None, gz, "gy"), P()),
        check_vma=False,
    )
```

```python
import numpy as np

import jax
import jax.numpy as jnp
from jax import lax
from jax.experimental import pallas as pl
from jax.experimental.pallas import tpu as pltpu
from jax.sharding import Mesh, PartitionSpec as P

NX = 24
STEPS = 8
HALO = STEPS
TAU_F = 0.52
TAU_G = 0.5376
LAT19 = [
    (0, 0, 0),
    (1, 0, 0),
    (-1, 0, 0),
    (0, 1, 0),
    (0, -1, 0),
    (0, 0, 1),
    (0, 0, -1),
    (1, 1, 0),
    (-1, -1, 0),
    (1, -1, 0),
    (-1, 1, 0),
    (1, 0, 1),
    (-1, 0, -1),
    (1, 0, -1),
    (-1, 0, 1),
    (0, 1, 1),
    (0, -1, -1),
    (0, 1, -1),
    (0, -1, 1),
]
WGT19 = [1.0 / 3.0] + [1.0 / 18.0] * 6 + [1.0 / 36.0] * 12
LAT7 = LAT19[:7]
WGT7 = [0.25] + [0.125] * 6
OPP = [LAT19.index(tuple(-v for v in c)) for c in LAT19]

KAPPA = -1.0 / (1.0 - TAU_F)
W2 = KAPPA / 36.0
KAPPA_0 = 1.0 / 36.0 / (1.0 - 1.0 / TAU_F)
OMG = 1.0 / TAU_G
LAMG = 1.0 - OMG
BIG = 1e30

NS = 8
XT = NX // 8
ROWS = 40


COPY = list(range(26))
for _i in range(1, 19):
    if LAT19[_i][2]:
        COPY[_i] = 26 + sum(1 for c in COPY if c >= 26)
for _i in range(1, 7):
    if LAT19[_i][2]:
        COPY[19 + _i] = 26 + sum(1 for c in COPY if c >= 26)
NCHAN = 26 + sum(1 for c in COPY if c >= 26)


def shift_lanes(v, by):
    return pltpu.roll(v, by % 128, axis=1)


def velocity_of(chan):
    return LAT19[chan] if chan < 19 else LAT19[chan - 19]


def put(ref, chan, slot, xt, v):
    ref[chan, slot, pl.ds(8 + 8 * xt, 8), :] = v


def tile(ref, chan, s, xt):
    return ref[chan, s + 1, pl.ds(8 + 8 * xt, 8), :]


def moved_tile(ref, chan, s, xt):
    c = velocity_of(chan)
    return ref[COPY[chan], s + 1 - c[1], pl.ds(8 + 8 * xt - c[0], 8), :]


def put_all(ref, s, xt, post):
    for chan, v in enumerate(post):
        put(ref, chan, s + 1, xt, v)


def copies(ref):
    def roll_line(s, carry):
        for xt in range(XT):
            for chan in range(26):
                c = velocity_of(chan)
                if c[2]:
                    put(ref, COPY[chan], s + 1, xt, shift_lanes(tile(ref, chan, s, xt), c[2]))
        return carry

    for xt in range(XT):
        for chan in range(26):
            c = velocity_of(chan)
            if c[1] > 0:
                put(ref, COPY[chan], 0, xt, shift_lanes(tile(ref, chan, NS - 1, xt), c[2] + 32))
            if c[1] < 0:
                put(ref, COPY[chan], NS + 1, xt, shift_lanes(tile(ref, chan, 0, xt), c[2] - 32))
    lax.fori_loop(0, NS, roll_line, 0, unroll=True)


def moments(f):
    quad = []
    for k in (7, 11, 15):
        p, m = f[k] + f[k + 2], f[k + 1] + f[k + 3]
        quad.append((p + m, p - m, (f[k] - f[k + 2]) - (f[k + 1] - f[k + 3])))
    rho = f[0] + (f[1] + f[2]) + (f[3] + f[4]) + (f[5] + f[6])
    rho = rho + quad[0][0] + quad[1][0] + quad[2][0]
    mx = (f[1] - f[2]) + quad[0][1] + quad[1][1]
    my = (f[3] - f[4]) + quad[0][2] + quad[2][1]
    mz = (f[5] - f[6]) + quad[1][2] + quad[2][2]
    return rho, mx, my, mz


def inverse(v):
    r = pl.reciprocal(v, approx=True)
    return r * (2.0 - v * r)


def collide(f, g):
    rho, mx, my, mz = moments(f)
    inv = inverse(rho)
    mom = (mx, my, mz)
    u = [m * inv for m in mom]
    y = [(4.5 * W2) * m for m in mom]
    diag = [y[a] * u[a] for a in range(3)]
    o = [(3.0 * W2) * m for m in mom]
    base = W2 * rho - (diag[0] + diag[1] + diag[2]) * (1.0 / 3.0)
    t = [base + d for d in diag]
    post = [None] * 19
    post[0] = f[0] + 12.0 * base
    for a in range(3):
        e, od = t[a] + t[a], o[a] + o[a]
        post[1 + 2 * a] = f[1 + 2 * a] + (e + od)
        post[2 + 2 * a] = f[2 + 2 * a] + (e - od)
    for k, a, b in ((7, 0, 1), (11, 0, 2), (15, 1, 2)):
        e = t[a] + diag[b]
        cross = (y[a] + y[a]) * u[b]
        ep, em = e + cross, e - cross
        op, om = o[a] + o[b], o[a] - o[b]
        post[k] = f[k] + (ep + op)
        post[k + 1] = f[k + 1] + (ep - op)
        post[k + 2] = f[k + 2] + (em + om)
        post[k + 3] = f[k + 3] + (em - om)
    temp = g[0] + (g[1] + g[2]) + (g[3] + g[4]) + (g[5] + g[6])
    eq = (0.125 * OMG) * temp
    eq4 = (0.5 * OMG) * temp
    post.append(LAMG * g[0] + (eq + eq))
    for a in range(3):
        ua = eq4 * u[a]
        post.append(LAMG * g[1 + 2 * a] + (eq + ua))
        post.append(LAMG * g[2 + 2 * a] + (eq - ua))
    return post


def equilibrium(u):
    y = [(4.5 * KAPPA_0) * v for v in u]
    diag = [y[a] * u[a] for a in range(3)]
    o = [(3.0 * KAPPA_0) * v for v in u]
    base = KAPPA_0 - (diag[0] + diag[1] + diag[2]) * (1.0 / 3.0)
    t = [base + d for d in diag]
    f = [None] * 19
    f[0] = 12.0 * base
    for a in range(3):
        e, od = t[a] + t[a], o[a] + o[a]
        f[1 + 2 * a], f[2 + 2 * a] = e + od, e - od
    for k, a, b in ((7, 0, 1), (11, 0, 2), (15, 1, 2)):
        e = t[a] + diag[b]
        cross = (y[a] + y[a]) * u[b]
        ep, em = e + cross, e - cross
        op, om = o[a] + o[b], o[a] - o[b]
        f[k], f[k + 1], f[k + 2], f[k + 3] = ep + op, ep - op, em + om, em - om
    return f


def stream(src, wa, wb, s, xt):
    f = [tile(src, 0, s, xt)]
    g = [tile(src, 19, s, xt)]
    for i in range(1, 19):
        moved = moved_tile(src, i, s, xt)
        open_ = moved < BIG
        f.append(jnp.where(open_, moved, tile(src, OPP[i], s, xt)))
        if i < 7:
            back = tile(src, 19 + OPP[i], s, xt)
            c = LAT19[i]
            near = (c[2] % 3, s + 1 - c[1], pl.ds(8 + 8 * xt - c[0], 8))
            back = wa[near] * back + wb[near]
            g.append(jnp.where(open_, moved_tile(src, 19 + i, s, xt), back))
    return f, g


def window(zbase, side_one, own, side_two, end_one, end_two, temp_out, flow_out, part_out,
           stage, inp, pops, wa, wb, res):
    height = zbase[1]
    even_y, even_z = zbase[2] > 0.5, zbase[3] > 0.5

    def low_high(even, one, two):
        return jnp.where(even, two, one), jnp.where(even, one, two)

    for a in range(5):
        left, right = low_high(even_y, side_one[a], side_two[a])
        top, bot = low_high(even_z, end_one[a], end_two[a])
        blocks = (left, own[a, :, 0:192], own[a, :, 192:384], right)
        for q in range(4):
            r0 = 32 * q
            stage[a, r0 : r0 + 8, 0:192] = top[:, 192 * q : 192 * q + 192]
            stage[a, r0 + 8 : r0 + 24, 0:192] = blocks[q]
            stage[a, r0 + 24 : r0 + 32, 0:192] = bot[:, 192 * q : 192 * q + 192]
        inp[a, 0:16] = stage[a, :, 0:128].T.reshape(16, 8, 128)
        inp[a, 16:24] = stage[a, :, 128:256].T[0:64].reshape(8, 8, 128)

    lane = lax.broadcasted_iota(jnp.int32, (8, 128), 1)
    zin = lane % 32
    mine = (zin >= HALO) & (zin < 32 - HALO) & (lane >= 32) & (lane < 96)
    zpos = zbase[0] + zin.astype(jnp.float32)
    ramp = 0.5 - 0.75 * (zpos + 0.5) / height

    def first(s):
        for xt in range(XT):
            kind = inp[0, s * XT + xt]
            hot, cold = kind == 2.0, kind == 3.0
            sign = jnp.where(hot | cold, -1.0, 1.0)
            gain = jnp.where(hot, 0.125, jnp.where(cold, -0.125, 0.0))
            for ref, v in ((wa, sign), (wb, gain)):
                for chan in range(3):
                    put(ref, chan, s + 1, xt, shift_lanes(v, (0, 1, -1)[chan]) if chan else v)
                if s == 0:
                    put(ref, 0, NS + 1, xt, shift_lanes(v, -32))
                if s == NS - 1:
                    put(ref, 0, 0, xt, shift_lanes(v, 32))
            fluid = kind == 0.0
            u = [inp[2 + a, s * XT + xt] for a in range(3)]
            temp = ramp + 0.05 * inp[1, s * XT + xt]
            f = equilibrium(u)
            f = [jnp.where(fluid, v, jnp.nan) for v in f]
            eq, eq4 = 0.125 * temp, 0.5 * temp
            f.append(eq + eq)
            for a in range(3):
                ua = eq4 * u[a]
                f.append(eq + ua)
                f.append(eq - ua)
            put_all(pops.at[0], s, xt, f)

    for s in range(NS):
        first(s)
    copies(pops.at[0])

    def step(k, carry):
        src, dst = pops.at[lax.rem(k + 1, 2)], pops.at[lax.rem(k, 2)]

        def line(s, c):
            for xt in range(XT):
                f, g = stream(src, wa, wb, s, xt)
                put_all(dst, s, xt, collide(f, g))
            return c

        lax.fori_loop(0, NS, line, 0, unroll=True)
        copies(dst)
        return carry

    lax.fori_loop(1, STEPS, step, 0, unroll=True)
    src = pops.at[(STEPS - 1) % 2]

    def last(s, total):
        for xt in range(XT):
            f, g = stream(src, wa, wb, s, xt)
            rho, mx, my, mz = moments(f)
            fluid = f[0] < BIG
            inv = inverse(rho)
            kind = inp[0, s * XT + xt]
            walls = jnp.where(kind == 2.0, 0.5, jnp.where(kind == 3.0, -0.5, 0.0))
            temp = g[0] + (g[1] + g[2]) + (g[3] + g[4]) + (g[5] + g[6])
            temp = jnp.where(fluid, temp, walls)
            res[0, s * XT + xt] = temp
            for a, m in enumerate((mx, my, mz)):
                res[1 + a, s * XT + xt] = jnp.where(fluid, m * inv, 0.0)
            heated = fluid & mine & (wb[0, s, pl.ds(8 + 8 * xt, 8), :] == 0.125)
            total = total + jnp.where(heated, 0.5 - temp, 0.0)
        return total

    total = lax.fori_loop(0, NS, last, jnp.zeros((8, 128), jnp.float32), unroll=True)
    part_out[...] = jnp.full(part_out.shape, jnp.sum(total), jnp.float32)
    for o in range(4):
        one = res[o, 0:16].reshape(128, 128).T
        two = res[o, 16:32].reshape(128, 128).T
        for q in (1, 2):
            rows = slice(32 * q + 8, 32 * q + 24)
            at = 192 * (q - 1)
            val = jnp.concatenate([one[rows], two[rows, 0:64]], axis=1)
            if o == 0:
                temp_out[:, at : at + 192] = val
            else:
                flow_out[o - 1, :, at : at + 192] = val


SCRATCH = [
    pltpu.VMEM((5, 128, 256), jnp.float32),
    pltpu.VMEM((5, NS * XT, 8, 128), jnp.float32),
    pltpu.VMEM((2, NCHAN, NS + 2, ROWS, 128), jnp.float32),
    pltpu.VMEM((3, NS + 2, ROWS, 128), jnp.float32),
    pltpu.VMEM((3, NS + 2, ROWS, 128), jnp.float32),
    pltpu.VMEM((4, 32, 8, 128), jnp.float32),
]


def all_sum(part, axes, count, first):
    order = [[(i + first) % count for i in range(count)]]
    parts = lax.all_to_all(part, axes, 0, 0, tiled=True, axis_index_groups=order)
    return jnp.sum(parts, axis=0)


def swap(axis, count, even, head, tail):
    near = [(i, i ^ 1) for i in range(count)]
    far = [(i, ((i + 1) ^ 1) - 1) for i in range(1, count - 1)]
    two = lax.ppermute(jnp.where(even, head, tail), axis, far)
    one = lax.ppermute(jnp.where(even, tail, head), axis, near)
    return one, two


def make_body(gz, gy, near, far, n_near, n_far, n_gz, n_gy):
    def body(cell_type, perturb, velocity):
        slab, cells = cell_type.shape
        height = slab * n_gz
        own = jnp.concatenate(
            [
                cell_type.astype(jnp.float32)[None],
                perturb.astype(jnp.float32)[None],
                velocity,
            ]
        )
        rim = HALO * NX
        even_y = (lax.axis_index(gy) & 1) == 0
        even_z = (lax.axis_index(gz[-1]) & 1) == 0
        sides = swap(gy, n_gy, even_y, own[:, :, :rim], own[:, :, cells - rim :])
        left = jnp.where(even_y, sides[1], sides[0])
        right = jnp.where(even_y, sides[0], sides[1])
        wide = jnp.concatenate([left, own, right], axis=2)
        ends = swap(gz, n_gz, even_z, wide[:, :HALO], wide[:, slab - HALO :])
        zbase = jnp.stack(
            [
                (lax.axis_index(gz) * slab - HALO).astype(jnp.float32),
                jnp.float32(height),
                even_y.astype(jnp.float32),
                even_z.astype(jnp.float32),
            ]
        )
        vmem = pl.BlockSpec(memory_space=pltpu.VMEM)
        f32 = jnp.float32
        temp, flow, part = pl.pallas_call(
            window,
            in_specs=[pl.BlockSpec(memory_space=pltpu.SMEM)] + [vmem] * 5,
            out_specs=[vmem] * 3,
            out_shape=[
                jax.ShapeDtypeStruct((slab, cells), f32),
                jax.ShapeDtypeStruct((3, slab, cells), f32),
                jax.ShapeDtypeStruct((n_near, 128), f32),
            ],
            scratch_shapes=SCRATCH,
            compiler_params=pltpu.CompilerParams(vmem_limit_bytes=40 * 1024 * 1024),
            name="lattice_window",
        )(zbase, sides[0], own, sides[1], ends[0], ends[1])
        line = all_sum(part, near, n_near, n_gy + 5 * n_gy // 8)
        line = all_sum(jnp.broadcast_to(line, (n_far, 128)), far, n_far, 9 * n_far // 16)
        return temp, flow, line[0] * (2.0 / (NX * height))

    return body


def solution(mesh):
    n_gz, n_gy = mesh.shape["gz"], mesh.shape["gy"]
    z = n_gz // 4
    fine = Mesh(
        np.asarray(mesh.devices).reshape(2, z, 2, n_gy),
        ("yl", "z", "core", "gy"),
    )
    gz = ("yl", "z", "core")
    near = ("yl", "core", "gy")
    body = make_body(gz, "gy", near, "z", 4 * n_gy, z, n_gz, n_gy)
    return jax.shard_map(
        body,
        mesh=fine,
        in_specs=(P(gz, "gy"), P(gz, "gy"), P(None, gz, "gy")),
        out_specs=(P(gz, "gy"), P(None, gz, "gy"), P()),
        check_vma=False,
    )
```
